512 devices in a mesh: narrow: 8 (over y), ep: 64 (over z, x, core).
Axes of the slice: x: 4, y: 8, z: 8, core: 2. Of those that a mesh axis runs over, the one named last changes fastest.
Arguments:
- queries: bfloat16 [2048, 128, 576], P('ep', 'narrow'), may hold values from -6 to 6
- trunk_cache: bfloat16 [128, 768, 576], P('ep'), may hold values from -6 to 6
- branch_cache: bfloat16 [128, 16, 32, 576], P('ep'), may hold values from -6 to 6
- visible: int32 [128, 16, 16], P('ep'), may hold values from 0 to 1, as said below
- branch_len: int32 [128, 16], P('ep'), may hold values from 1 to 32, as said below
- value_up: bfloat16 [128, 512, 128], P('narrow'), may hold values from -0.25 to 0.25
- out_proj: bfloat16 [16384, 7168], P('narrow', 'ep'), may hold values from -0.1875 to 0.1875
- residual_in: bfloat16 [2048, 7168], P('narrow', 'ep'), may hold values from -4 to 4
- norm_gain: float32 [7168], replicated, may hold values from 0.25 to 1.75
- expert_ids: int32 [2048, 8], P('narrow'), may hold values from 0 to 255, all different within a row; in each aligned block of 256 rows (0 to 255, 256 to 511, ...) at most 16 rows name the same one
Outputs:
- hidden: bfloat16 [2048, 7168], P('narrow', 'ep')
- expert_inputs: bfloat16 [8, 256, 16, 7168], P('narrow', 'ep')
The draws below stay inside these ranges and needn't reach their ends.
Inputs may be any that keep to these rules, and one draw needn't show every extreme that they name: visible[r, b, b] = 1, branch 0 is the root of its tree, and the ones of a row are b and its chain of ancestors. `branch_len`: every tree has a branch of exactly 32 positions. `expert_ids`: within one block of 256 tokens no expert is chosen more than 16 times.
All inputs are finite; a program needn't handle non-finite values.
Results may differ from the reference program's by a relative error of at most 0.0066.
Values may be sent and summed in bfloat16 or wider, within the bound.
A program may use at most 64 MiB of HBM per device.

```python
import math
import jax
import jax.numpy as jnp
import numpy as np
from jax import lax

D = 7168
HEADS = 128
LAT = 512
VDIM = 128
TOP = 8
BRANCHES = 16
TRUNK = 768
BRMOST = 32
KDIM = 576
TREES = 128
TOKENS = 2048
EXPERTS = 256
BLOCK_ROWS = 256
SLOTS = 16
N_NARROW = 8


def draw_queries(key, part):
    key = jax.random.fold_in(key, 31)
    values = jnp.clip(jax.random.normal(key, (TOKENS, HEADS, KDIM), jnp.float32), -6.0, 6.0)
    return values.astype(jnp.bfloat16)


def draw_trunk_cache(key, part):
    key = jax.random.fold_in(key, 37)
    values = jnp.clip(jax.random.normal(key, (TREES, TRUNK, KDIM), jnp.float32), -6.0, 6.0)
    return values.astype(jnp.bfloat16)


def draw_visible(key, part):
    key = jax.random.fold_in(key, 11)
    raw = jax.random.randint(key, (TREES, BRANCHES), 0, 1 << 20)
    below = jnp.maximum(jnp.arange(BRANCHES, dtype=jnp.int32), 1)
    parent = raw % below[None, :]
    current = jnp.broadcast_to(jnp.arange(BRANCHES, dtype=jnp.int32)[None, :], (TREES, BRANCHES))
    marks = current[:, :, None] == jnp.arange(BRANCHES, dtype=jnp.int32)[None, None, :]
    for step in range(BRANCHES):
        current = jnp.take_along_axis(parent, current, axis=1)
        marks = marks | (current[:, :, None] == jnp.arange(BRANCHES, dtype=jnp.int32)[None, None, :])
    return marks.astype(jnp.int32)


def draw_branch_len(key, part):
    key = jax.random.fold_in(key, 23)
    first, second = jax.random.split(key)
    length = jax.random.randint(first, (TREES, BRANCHES), 1, BRMOST + 1)
    pick = jax.random.randint(second, (TREES, 1), 0, BRANCHES)
    full = jnp.arange(BRANCHES, dtype=jnp.int32)[None, :] == pick
    return jnp.where(full, BRMOST, length).astype(jnp.int32)


def block_levels(key, extent, cuts, low, high):
    gain = 1.0
    for dim, shards_of in cuts:
        heights = jax.random.uniform(jax.random.fold_in(jax.random.fold_in(key, 6), dim), (shards_of,), jnp.float32, low / len(cuts), high / len(cuts))
        gain = gain * jnp.repeat(jnp.exp(heights), extent[dim] // shards_of).reshape((-1,) + (1,) * (len(extent) - 1 - dim))
    return gain


def shared_out(stream_key, own, number, rows, count, top, most, skew):
    sequence = jax.random.permutation(stream_key, count)
    heavy_load, ordinary = portions_of(count, rows * top, most, skew, True), portions_of(count, rows * top, most, skew, False)
    places = jnp.arange(count)

    def named(sizes, rotation):
        used = int((sizes > 0).sum())
        fixed = max(1, used // 4)
        shifted = fixed + (places - fixed + rotation * (used - fixed)) % max(1, count - fixed)
        return jnp.zeros((count,), jnp.int32).at[sequence[jnp.where(places < fixed, places, shifted)]].set(jnp.asarray(sizes, jnp.int32))

    sizes = jnp.where(number % 4 == 0, named(heavy_load, number // 4), named(ordinary, number - number // 4 - 1))
    mixed = jax.random.permutation(jax.random.fold_in(own, 3), count)
    giver, taker = mixed[0:count // 2 * 2:2], mixed[1:count // 2 * 2:2]
    room = jnp.minimum(sizes[giver] - 1, most - sizes[taker]) // 2
    room = jnp.where((giver == sequence[0]) | (taker == sequence[0]) | (sizes[taker] == 0), 0, jnp.maximum(room, 0))
    shifted = jax.random.randint(jax.random.fold_in(own, 4), (count // 2,), 0, 1 << 20) % (room + 1)
    sizes = sizes.at[giver].add(-shifted).at[taker].add(shifted)
    items = jnp.searchsorted(jnp.cumsum(sizes), jnp.arange(rows * top), side="right").astype(jnp.int32)
    table = items.reshape(top, rows).T
    table = table[jax.random.permutation(jax.random.fold_in(own, 1), rows)]
    rotation = jax.random.randint(jax.random.fold_in(own, 2), (rows, 1), 0, top)
    return jnp.take_along_axis(table, (jnp.arange(top)[None, :] + rotation) % top, axis=1)


def portions_of(amount, total, bound, skew, full):
    loads = [(1 << 20) // math.isqrt(standing ** skew) + 1 for standing in range(1, amount + 1)]
    largest = bound if full else min(bound, max(-(-total // amount), total * loads[0] // sum(loads)))
    least = 1 if total - largest >= amount - 1 else 0
    given, spare = [largest] + [least] * (amount - 1), total - largest - least * (amount - 1)
    while spare > 0:
        candidates = [i for i in range(1, amount) if given[i] < largest] or [i for i in range(1, amount) if given[i] < bound]
        pool, remaining = sum([loads[i] for i in candidates]), spare
        for i in candidates:
            addition = min(bound - given[i], max(1, remaining * loads[i] // pool), spare)
            given[i] = given[i] + addition
            spare = spare - addition
    return np.array(given)


def bell_draw(key, dims, width, limit, pieces=(), held_as=jnp.bfloat16):
    result = jax.random.normal(key, dims, jnp.float32) * width
    if len(pieces) > 0:
        result = block_levels(key, dims, pieces, -0.22, 0.18) * result
    return jnp.clip(result, min=-limit, max=limit).astype(held_as)


def setup_inputs(seed: int = 0) -> dict:
    key_of = jax.random.split(jax.random.key(seed), 11)
    queries = draw_queries(jax.random.fold_in(key_of[10], 71), 0)
    trunk_cache = draw_trunk_cache(jax.random.fold_in(key_of[10], 71), 0)
    branch_cache = bell_draw(key_of[2], (TREES, BRANCHES, BRMOST, KDIM), 1.0, 6.0, ((0, 64),))
    visible = draw_visible(jax.random.fold_in(key_of[10], 71), 0)
    branch_len = draw_branch_len(jax.random.fold_in(key_of[10], 71), 0)
    value_up = bell_draw(key_of[5], (HEADS, LAT, VDIM), LAT ** -0.5, 0.25, ((0, 8),))
    out_proj = bell_draw(key_of[6], (HEADS * VDIM, D), (HEADS * VDIM // 16) ** -0.5, 0.1875, ((0, 8), (1, 64)))
    residual_in = bell_draw(key_of[7], (TOKENS, D), 0.5, 4.0, ((0, 8), (1, 64)))
    norm_gain = jnp.clip(1.0 + 0.15 * jax.random.normal(key_of[8], (D,), jnp.float32), 0.25, 1.75)
    expert_ids_keys = jax.random.split(jax.random.fold_in(key_of[9], 1), TOKENS // BLOCK_ROWS)
    expert_ids_turns = jax.random.permutation(jax.random.fold_in(key_of[9], 3), TOKENS // BLOCK_ROWS)
    expert_ids = jax.vmap(lambda own, number: shared_out(jax.random.fold_in(key_of[9], 2), own, number, BLOCK_ROWS, EXPERTS, TOP, SLOTS, 2))(expert_ids_keys, expert_ids_turns).reshape((TOKENS, TOP))
    return {"queries": queries, "trunk_cache": trunk_cache, "branch_cache": branch_cache, "visible": visible, "branch_len": branch_len, "value_up": value_up, "out_proj": out_proj, "residual_in": residual_in, "norm_gain": norm_gain, "expert_ids": expert_ids}


score_scale = 192.0 ** (-0.5)
norm_eps = 1e-06

def tree_attention(query, trunk, branch, visible, length):
    keys = branch.reshape(BRANCHES * BRMOST, KDIM)
    query_f = query.astype(jnp.float32)
    trunk_scores = jnp.einsum('bhk,pk->bhp', query_f, trunk.astype(jnp.float32)) * score_scale
    branch_scores = jnp.einsum('bhk,pk->bhp', query_f, keys.astype(jnp.float32)) * score_scale
    position = jnp.arange(BRMOST, dtype=jnp.int32)
    live = (visible[:, :, None] > 0) & (position[None, None, :] < length[None, :, None])
    live = live.reshape(BRANCHES, 1, BRANCHES * BRMOST)
    branch_scores = jnp.where(live, branch_scores, -jnp.inf)
    scores = jnp.concatenate([trunk_scores, branch_scores], axis=-1)
    top_score = lax.optimization_barrier(jnp.max(scores, axis=-1, keepdims=True))
    expo = jnp.exp(scores - top_score)
    weights = (expo / lax.optimization_barrier(jnp.sum(expo, axis=-1, keepdims=True))).astype(jnp.bfloat16)
    values = jnp.concatenate([trunk[:, :LAT], keys[:, :LAT]], axis=0)
    latent_out = jnp.einsum('bhp,pl->bhl', weights.astype(jnp.float32), values.astype(jnp.float32))
    return latent_out.astype(jnp.bfloat16)

def reference(queries, trunk_cache, branch_cache, visible, branch_len, value_up, out_proj, residual_in, norm_gain, expert_ids):
    grouped = queries.reshape(TREES, BRANCHES, HEADS, KDIM)

    def per_tree(items):
        latent_out = tree_attention(*items)
        feats = jnp.einsum('bhl,hlv->bhv', latent_out.astype(jnp.float32), value_up.astype(jnp.float32))
        return feats.astype(jnp.bfloat16).reshape(BRANCHES, HEADS * VDIM)
    features = lax.map(per_tree, (grouped, trunk_cache, branch_cache, visible, branch_len))
    features = features.reshape(TOKENS, HEADS * VDIM)
    projected = jnp.dot(features, out_proj, preferred_element_type=jnp.float32)
    hidden = (residual_in.astype(jnp.float32) + projected).astype(jnp.bfloat16)
    hidden_f = hidden.astype(jnp.float32)
    mean_square = lax.optimization_barrier(jnp.mean(hidden_f * hidden_f, axis=-1, keepdims=True))
    normed = (hidden_f * lax.rsqrt(mean_square + norm_eps) * norm_gain[None, :]).astype(jnp.bfloat16)

    def place(items):
        ids, rows = items
        onehot = (ids[:, None] == jnp.arange(EXPERTS, dtype=jnp.int32)[None, :]).astype(jnp.int32)
        before = jnp.cumsum(onehot, axis=0) - onehot
        slot = lax.optimization_barrier(jnp.sum(before * onehot, axis=1))
        target = ids * SLOTS + slot
        source = jnp.arange(BLOCK_ROWS * TOP, dtype=jnp.int32) // TOP
        placed = jnp.zeros((EXPERTS * SLOTS, D), jnp.bfloat16).at[target].set(rows[source])
        return placed.reshape(EXPERTS, SLOTS, D)
    expert_inputs = lax.map(place, (expert_ids.reshape(N_NARROW, BLOCK_ROWS * TOP), normed.reshape(N_NARROW, BLOCK_ROWS, D)))
    return (hidden, expert_inputs)
```

```python
import functools

import jax
import jax.numpy as jnp
from jax import lax
from jax.experimental import pallas as pl
from jax.experimental.pallas import tpu as pltpu
from jax.sharding import PartitionSpec as P

NX = 4
GROUP = 2 * NX
EXP_DEV = 4
SLOTS = 16

score_scale = 192.0 ** (-0.5)
norm_eps = 1e-06

MESH = pl.DeviceIdType.MESH
NT = (((1,), (1,)), ((), ()))
NN = (((1,), (0,)), ((), ()))


def matmul(a, b, dims=NN):
    return lax.dot_general(a, b, dims, preferred_element_type=jnp.float32)


class Ids:
    def __init__(self):
        self.names = {}

    def __call__(self, *name):
        return self.names.setdefault(name, len(self.names))


def kernel(
    cfg,
    q_hbm,
    trunk_hbm,
    branch_hbm,
    vup_hbm,
    w_hbm,
    vis_ref,
    len_ref,
    res_ref,
    gain_ref,
    ids_ref,
    hid_ref,
    out_ref,
    q_ref,
    trunk_ref,
    branch_ref,
    vup_ref,
    s_ref,
    p_ref,
    bias_ref,
    lat_ref,
    feat_ref,
    w_ref,
    rt_ref,
    rb_ref,
    part_ref,
    part16_ref,
    got_ref,
    h_ref,
    onehot_ref,
    picked_ref,
    in_sem,
    send_sem,
    recv_sem,
):
    ny, nz, sem_count = cfg
    trees, rows, kdim = q_ref.shape
    trunk_len = trunk_ref.shape[2]
    nkeys = branch_ref.shape[1]
    heads, lat, vdim = vup_ref.shape
    branches = vis_ref.shape[1]
    brmost = nkeys // branches
    cols = w_hbm.shape[0]
    cz = GROUP * cols
    toks = trees * branches
    block = GROUP * toks
    width = nz * cz
    bf16, f32, i32 = jnp.bfloat16, jnp.float32, jnp.int32

    y = lax.axis_index("narrow")
    ep = lax.axis_index("ep")
    z = ep // GROUP
    j = ep % GROUP
    x = j // 2
    core = j % 2

    def at(dy=0, dz=0, dx=0, flip=False):
        yy = (y + dy) % ny
        zz = (z + dz) % nz
        xx = (x + dx) % NX
        cc = 1 - core if flip else core
        return (yy, zz * GROUP + xx * 2 + cc)

    barrier = pltpu.get_barrier_semaphore()
    partners = [at(dz=1), at(dz=-1)]
    partners += [(y, z * GROUP + (j + k) % GROUP) for k in range(1, GROUP)]
    partners += [at(dy=d) for d in range(1, ny)]
    for p in partners:
        pl.semaphore_signal(barrier, inc=1, device_id=p, device_id_type=MESH)

    loads = []

    def load(src, dst):
        c = pltpu.make_async_copy(src, dst, in_sem.at[len(loads)])
        c.start()
        loads.append(c)
        return c

    def w_rows(jj, lo=0, hi=None):
        hi = cols if hi is None else hi
        return w_ref.at[pl.ds(pl.multiple_of(jj * cols + lo, 16), hi - lo), :]

    tree_loads = []
    for t in range(trees):
        tree_loads.append(
            [
                load(q_hbm.at[t], q_ref.at[t]),
                load(trunk_hbm.at[t], trunk_ref.at[t]),
                load(branch_hbm.at[t], branch_ref.at[t]),
            ]
        )
    vup_load = load(vup_hbm, vup_ref)
    own_w = load(w_hbm, w_rows(j))

    res = res_ref[...]
    fill = 128 - cols
    if fill:
        res = jnp.concatenate([res, jnp.zeros((fill, block), bf16)], axis=0)
    ri = lax.broadcasted_iota(i32, (block, block), 0)
    ci = lax.broadcasted_iota(i32, (block, block), 1)
    eye = (ri == ci).astype(f32).astype(bf16)
    rt_ref[...] = matmul(eye, res, NT).astype(bf16).reshape(GROUP, toks, 128)

    sends = []
    ids = Ids()

    def copy(name, src, dst, dev):
        i = ids(*name)
        c = pltpu.make_async_remote_copy(
            src_ref=src,
            dst_ref=dst,
            send_sem=send_sem.at[i],
            recv_sem=recv_sem.at[i],
            device_id=dev,
            device_id_type=MESH,
        )
        c.start()
        sends.append(c)

    def arrived(name, dst):
        i = ids(*name)
        pltpu.make_async_remote_copy(
            src_ref=dst,
            dst_ref=dst,
            send_sem=send_sem.at[i],
            recv_sem=recv_sem.at[i],
            device_id=at(flip=True),
            device_id_type=MESH,
        ).wait_recv()

    pl.semaphore_wait(barrier, len(partners))

    wsplit = (cols // 16 + 1) // 2 * 16
    copy(("w", 1), w_hbm, w_rows(j), at(dx=1))
    copy(("w", -1), w_hbm, w_rows(j), at(dx=-1))
    copy(("ws", 0), w_hbm, w_rows(j), at(flip=True))
    for k in range(1, GROUP):
        jj = (j + k) % GROUP
        copy(("r", k), rt_ref.at[jj], rb_ref.at[j], (y, z * GROUP + jj))

    def xj(dx):
        return ((x + dx) % NX) * 2 + core

    def xj_other(dx):
        return ((x + dx) % NX) * 2 + (1 - core)

    for t in range(trees):
        for c in tree_loads[t]:
            c.wait()
        key_i = lax.broadcasted_iota(i32, (branches, nkeys), 1)
        owner = key_i // brmost
        pos = key_i % brmost
        vis = jnp.zeros((branches, nkeys), i32)
        lim = jnp.zeros((branches, nkeys), i32)
        for b in range(branches):
            here = owner == b
            vis = jnp.where(here, vis_ref[t, :, b : b + 1], vis)
            lim = jnp.where(here, len_ref[t : t + 1, b : b + 1], lim)
        live = (vis > 0) & (pos < lim)
        bias_ref[...] = jnp.where(live, 0.0, -1e30)

        q = q_ref[t]
        s_ref[:, :trunk_len] = matmul(q, trunk_ref[t])
        s_ref[:, trunk_len:] = matmul(q, branch_ref[t], NT)

        def soft(b, carry):
            r = pl.ds(pl.multiple_of(b * heads, heads), heads)
            st = s_ref[r, :trunk_len] * score_scale
            sb = s_ref[r, trunk_len:] * score_scale + bias_ref[pl.ds(b, 1), :]
            top = jnp.maximum(
                jnp.max(st, axis=-1, keepdims=True), jnp.max(sb, axis=-1, keepdims=True)
            )
            et = jnp.exp(st - top)
            eb = jnp.exp(sb - top)
            inv = 1.0 / (
                jnp.sum(et, axis=-1, keepdims=True) + jnp.sum(eb, axis=-1, keepdims=True)
            )
            p_ref[r, :trunk_len] = (et * inv).astype(bf16)
            p_ref[r, trunk_len:] = (eb * inv).astype(bf16)
            return carry

        lax.fori_loop(0, branches, soft, 0, unroll=4)
        o = matmul(p_ref[:, :trunk_len], trunk_ref[t, :lat, :], NT)
        o = o + matmul(p_ref[:, trunk_len:], branch_ref[t, :, :lat])
        o = o.astype(bf16)
        ro = lax.broadcasted_iota(i32, (rows, rows), 0)
        co = lax.broadcasted_iota(i32, (rows, rows), 1)
        swap = (co == (ro % branches) * heads + ro // branches).astype(f32).astype(bf16)
        o = matmul(swap, o).astype(bf16)
        lat_ref[:, t * branches : (t + 1) * branches, :] = o.reshape(heads, branches, lat)

    vup_load.wait()
    for h in range(heads):
        f = matmul(lat_ref[h], vup_ref[h])
        feat_ref[0, :, h * vdim : (h + 1) * vdim] = f.astype(bf16)

    half_z = nz // 2
    mid = toks // 2

    def f_part(slot, step, way):
        if step == half_z:
            return feat_ref.at[slot, (slice(0, mid) if way > 0 else slice(mid, toks)), :]
        return feat_ref.at[slot]

    def f_send(step):
        for way in (1, -1):
            src = (-way * (step - 1)) % nz
            dst = (-way * step) % nz
            copy(("f", way, step), f_part(src, step, way), f_part(dst, step, way), at(dz=way))

    def f_wait(step):
        for way in (1, -1):
            arrived(("f", way, step), f_part((-way * step) % nz, step, way))

    f_send(1)

    id_rows = ids_ref[...]
    marks = jnp.zeros((16, block), f32)
    mrow = lax.broadcasted_iota(i32, (16, block), 0)
    for e in range(EXP_DEV):
        hit = jnp.where(id_rows == ep * EXP_DEV + e, 1.0, 0.0)
        hit = jnp.sum(hit, axis=0, keepdims=True)
        marks = jnp.where(mrow == e, hit, marks)
    earlier = (ri < ci).astype(f32).astype(bf16)
    before = matmul(marks.astype(bf16), earlier)
    srow = lax.broadcasted_iota(i32, (SLOTS, block), 0).astype(f32)
    for e in range(EXP_DEV):
        chosen = (before[e : e + 1, :] == srow) & (marks[e : e + 1, :] > 0.5)
        onehot_ref[e * SLOTS : (e + 1) * SLOTS, :] = jnp.where(chosen, 1.0, 0.0).astype(bf16)

    f_wait(1)
    f_send(2)

    arrived(("w", 1), w_rows(xj(-1)))
    copy(("w2", 1), w_rows(xj(-1), 0, wsplit), w_rows(xj(-1), 0, wsplit), at(dx=1))
    copy(("ws", 1), w_rows(xj(-1)), w_rows(xj(-1)), at(flip=True))
    arrived(("w", -1), w_rows(xj(1)))
    copy(("w2", -1), w_rows(xj(1), wsplit), w_rows(xj(1), wsplit), at(dx=-1))
    copy(("ws", -1), w_rows(xj(1)), w_rows(xj(1)), at(flip=True))

    for step in range(3, half_z + 1):
        f_wait(step - 1)
        f_send(step)

    arrived(("w2", 1), w_rows(xj(2), 0, wsplit))
    copy(("ws2", 1), w_rows(xj(2), 0, wsplit), w_rows(xj(2), 0, wsplit), at(flip=True))
    arrived(("w2", -1), w_rows(xj(2), wsplit))
    copy(("ws2", -1), w_rows(xj(2), wsplit), w_rows(xj(2), wsplit), at(flip=True))

    rb_ref[j] = rt_ref[j]
    for k in range(1, GROUP):
        arrived(("r", k), rb_ref.at[(j + GROUP - k) % GROUP])
    residual = jnp.concatenate(
        [rb_ref[g].astype(f32)[:, :cols] for g in range(GROUP)], axis=1
    )

    own_w.wait()
    arrived(("ws", 0), w_rows(xj_other(0)))
    arrived(("ws", 1), w_rows(xj_other(-1)))
    arrived(("ws", -1), w_rows(xj_other(1)))
    arrived(("ws2", 1), w_rows(xj_other(2), 0, wsplit))
    arrived(("ws2", -1), w_rows(xj_other(2), wsplit))
    f_wait(half_z)

    feats = feat_ref[...].reshape(nz * toks, heads * vdim)
    for lo in range(0, cz, 256):
        hi = min(cz, lo + 256)
        prod = matmul(feats, w_ref[lo:hi, :], NT)
        part_ref[:, lo:hi] = prod
        part16_ref[:, lo:hi] = prod.astype(bf16)

    def part_rows(ref, dy):
        slot = (y + dy - z + nz) % nz
        return ref.at[pl.ds(pl.multiple_of(slot * toks, 16), toks), :]

    for d in range(1, ny):
        copy(("p", d), part_rows(part16_ref, d), got_ref.at[d - 1], at(dy=d))
    total = residual
    own = part_rows(part_ref, 0)[...]
    for d in range(1, ny):
        arrived(("p", d), got_ref.at[d - 1])
        own = own + got_ref[d - 1].astype(f32)
    hidden = (total + own).astype(bf16)

    zsplit = (cz // 128 + 1) // 2 * 128
    xsplit = width // 2

    def z_cols(dz, lo=0, hi=None):
        hi = cz if hi is None else hi
        return pl.ds(pl.multiple_of(((z + dz + nz) % nz) * cz + lo, 128), hi - lo)

    def xx(dx):
        return (x + dx + NX) % NX

    h_ref[x, core, 0, :, z_cols(0)] = hidden[:16]
    h_ref[x, core, 1, :, z_cols(0)] = hidden[16:]

    def piece(way):
        return (0, zsplit) if way > 0 else (zsplit, cz)

    def a1(step, way, cc=core):
        lo, hi = piece(way) if step == half_z else (0, cz)
        return lambda dz: h_ref.at[x, cc, 0, :, z_cols(dz, lo, hi)]

    def a1_send(step):
        for way in (1, -1):
            s = a1(step, way)(-way * (step - 1))
            copy(("a1", way, step), s, s, at(dz=way))

    def a1_wait(step):
        for way in (1, -1):
            arrived(("a1", way, step), a1(step, way)(-way * step))

    def b2(step, way, cc):
        lo, hi = piece(way) if step == half_z else (0, cz)
        return lambda dz: h_ref.at[:, cc, 1, :, z_cols(dz, lo, hi)]

    def b2_send(step):
        for way in (1, -1):
            s = b2(step, way, core)(-way * (step - 1))
            copy(("b2", way, step), s, s, at(dz=way))

    def b2_wait(step):
        for way in (1, -1):
            s = b2(step, way, core)(-way * step)
            arrived(("b2", way, step), s)
            copy(("bs", way, step), s, s, at(flip=True))

    def b1(dx, lo=0, hi=None):
        return h_ref.at[xx(dx), core, 1, :, z_cols(0, lo, hi)]

    def a2(dx, cc, lo=0, hi=None):
        hi = width if hi is None else hi
        return h_ref.at[xx(dx), cc, 0, :, lo:hi]

    a1_send(1)
    for way in (1, -1):
        copy(("b1", way), b1(0), b1(0), at(dx=way))
    for way in (1, -1):
        arrived(("b1", way), b1(-way))
        s = b1(-way, *piece(way))
        copy(("b1r", way), s, s, at(dx=way))
    a1_wait(1)
    a1_send(2)
    for way in (1, -1):
        arrived(("b1r", way), b1(-2 * way, *piece(way)))
    b2_send(1)
    s = b2(0, 1, core)(0)
    copy(("bs", 0), s, s, at(flip=True))
    for step in range(3, half_z + 1):
        a1_wait(step - 1)
        a1_send(step)
    a1_wait(half_z)
    for way in (1, -1):
        copy(("a2", way), a2(0, core), a2(0, core), at(dx=way))
    copy(("as", 0), a2(0, core), a2(0, core), at(flip=True))
    b2_wait(1)
    b2_send(2)

    def x_half(way):
        return (0, xsplit) if way > 0 else (xsplit, width)

    for way in (1, -1):
        arrived(("a2", way), a2(-way, core))
        s = a2(-way, core, *x_half(way))
        copy(("a2r", way), s, s, at(dx=way))
        s = a2(-way, core)
        copy(("as", way), s, s, at(flip=True))
    for step in range(3, half_z + 1):
        b2_wait(step - 1)
        b2_send(step)
    for way in (1, -1):
        s = a2(-2 * way, core, *x_half(way))
        arrived(("a2r", way), s)
        copy(("as2", way), s, s, at(flip=True))
    b2_wait(half_z)

    other = 1 - core
    arrived(("bs", 0), b2(0, 1, other)(0))
    arrived(("as", 0), a2(0, other))
    for way in (1, -1):
        arrived(("as", way), a2(-way, other))
        arrived(("as2", way), a2(-2 * way, other, *x_half(way)))
        for step in range(1, half_z + 1):
            arrived(("bs", way, step), b2(step, way, other)(-way * step))

    si = lax.broadcasted_iota(i32, (cols, cz), 0)
    sc = lax.broadcasted_iota(i32, (cols, cz), 1)
    mine = (sc == si + j * cols).astype(f32).astype(bf16)
    hz = h_ref[:, :, :, :, z_cols(0)].reshape(block, cz)
    hid_ref[...] = matmul(mine, hz, NT).astype(bf16)

    chosen = onehot_ref[...]
    squares = jnp.zeros((EXP_DEV * SLOTS, 1), f32)
    for g in range(nz):
        rows_in = h_ref[:, :, :, :, g * cz : (g + 1) * cz].reshape(block, cz)
        got = matmul(chosen, rows_in)
        picked_ref[:, g * cz : (g + 1) * cz] = got
        squares = squares + jnp.sum(got * got, axis=-1, keepdims=True)
    scale = lax.rsqrt(squares / width + norm_eps)
    for g in range(nz):
        c = slice(g * cz, (g + 1) * cz)
        out_ref[:, c] = (picked_ref[:, c] * scale * gain_ref[:, c]).astype(bf16)

    for c in sends:
        c.wait_send()
    assert len(ids.names) <= sem_count


def shards(
    queries,
    trunk_cache,
    branch_cache,
    visible,
    branch_len,
    value_up,
    out_proj,
    residual_in,
    norm_gain,
    expert_ids,
):
    ny = lax.axis_size("narrow")
    nz = lax.axis_size("ep") // GROUP
    trees, branches = branch_len.shape
    heads, lat, vdim = value_up.shape
    kdim = queries.shape[2]
    trunk_len = trunk_cache.shape[1]
    nkeys = branches * branch_cache.shape[2]
    feat, cols = out_proj.shape
    block = residual_in.shape[0]
    toks = trees * branches
    rows = branches * heads
    cz = GROUP * cols
    width = nz * cz
    bf16, f32 = jnp.bfloat16, jnp.float32
    sem_count = 96
    hbm = pl.BlockSpec(memory_space=pl.ANY)
    vmem = pl.BlockSpec(memory_space=pltpu.VMEM)
    chosen = EXP_DEV * SLOTS
    hidden, rows_out = pl.pallas_call(
        functools.partial(kernel, (ny, nz, sem_count)),
        out_shape=(
            jax.ShapeDtypeStruct((cols, block), bf16),
            jax.ShapeDtypeStruct((chosen, width), bf16),
        ),
        in_specs=[hbm] * 5 + [vmem] * 5,
        out_specs=(vmem, vmem),
        scratch_shapes=[
            pltpu.VMEM((trees, rows, kdim), bf16),
            pltpu.VMEM((trees, kdim, trunk_len), bf16),
            pltpu.VMEM((trees, nkeys, kdim), bf16),
            pltpu.VMEM((heads, lat, vdim), bf16),
            pltpu.VMEM((rows, trunk_len + nkeys), f32),
            pltpu.VMEM((rows, trunk_len + nkeys), bf16),
            pltpu.VMEM((branches, nkeys), f32),
            pltpu.VMEM((heads, toks, lat), bf16),
            pltpu.VMEM((nz, toks, feat), bf16),
            pltpu.VMEM((cz, feat), bf16),
            pltpu.VMEM((GROUP, toks, 128), bf16),
            pltpu.VMEM((GROUP, toks, 128), bf16),
            pltpu.VMEM((nz * toks, cz), f32),
            pltpu.VMEM((nz * toks, cz), bf16),
            pltpu.VMEM((ny - 1, toks, cz), bf16),
            pltpu.VMEM((NX, 2, 2, 16, width), bf16),
            pltpu.VMEM((chosen, block), bf16),
            pltpu.VMEM((chosen, width), f32),
            pltpu.SemaphoreType.DMA((16,)),
            pltpu.SemaphoreType.DMA((sem_count,)),
            pltpu.SemaphoreType.DMA((sem_count,)),
        ],
        compiler_params=pltpu.CompilerParams(
            collective_id=0, has_side_effects=True, vmem_limit_bytes=48 * 1024 * 1024
        ),
        name="decode_layer",
    )(
        queries.reshape(trees, rows, kdim),
        jnp.swapaxes(trunk_cache, 1, 2),
        branch_cache.reshape(trees, nkeys, kdim),
        value_up,
        out_proj.T,
        visible,
        branch_len,
        residual_in.T,
        norm_gain.reshape(1, width),
        expert_ids.T,
    )
    return hidden.T, rows_out.reshape(1, EXP_DEV, SLOTS, width)


def solution(mesh):
    placed = (
        P("ep", "narrow", None),
        P("ep", None, None),
        P("ep", None, None, None),
        P("ep", None, None),
        P("ep", None),
        P("narrow", None, None),
        P("narrow", "ep"),
        P("narrow", "ep"),
        P(),
        P("narrow", None),
    )
    return jax.shard_map(
        shards,
        mesh=mesh,
        in_specs=placed,
        out_specs=(P("narrow", "ep"), P("narrow", "ep", None, None)),
        check_vma=False,
    )
```

```python
import functools

import jax
import jax.numpy as jnp
from jax import lax
from jax.experimental import pallas as pl
from jax.experimental.pallas import tpu as pltpu
from jax.sharding import PartitionSpec as P

NX = 4
GROUP = 2 * NX
EXP_DEV = 4
SLOTS = 16

score_scale = 192.0 ** (-0.5)
norm_eps = 1e-06

MESH = pl.DeviceIdType.MESH
NT = (((1,), (1,)), ((), ()))
NN = (((1,), (0,)), ((), ()))


def matmul(a, b, dims=NN):
    return lax.dot_general(a, b, dims, preferred_element_type=jnp.float32)


class Ids:
    def __init__(self):
        self.names = {}

    def __call__(self, *name):
        return self.names.setdefault(name, len(self.names))


def kernel(
    cfg,
    q_hbm,
    trunk_hbm,
    branch_hbm,
    vup_hbm,
    w_hbm,
    vis_hbm,
    len_hbm,
    res_hbm,
    gain_hbm,
    ids_hbm,
    hid_ref,
    out_ref,
    q_ref,
    trunk_ref,
    branch_ref,
    vup_ref,
    vis_ref,
    len_ref,
    res_ref,
    gain_ref,
    ids_ref,
    s_ref,
    p_ref,
    bias_ref,
    lat_ref,
    feat_ref,
    w_ref,
    rt_ref,
    rb_ref,
    part_ref,
    part16_ref,
    got_ref,
    sum_ref,
    h_ref,
    onehot_ref,
    picked_ref,
    in_sem,
    send_sem,
    recv_sem,
):
    ny, nz, sem_count = cfg
    trees, rows, kdim = q_ref.shape
    trunk_len = trunk_ref.shape[2]
    nkeys = branch_ref.shape[1]
    heads, lat, vdim = vup_ref.shape
    branches = vis_ref.shape[1]
    brmost = nkeys // branches
    cols = w_hbm.shape[0]
    cz = GROUP * cols
    toks = trees * branches
    block = GROUP * toks
    width = nz * cz
    bf16, f32, i32 = jnp.bfloat16, jnp.float32, jnp.int32
    REL = [0] + [w * d for d in range(1, nz // 2) for w in (1, -1)] + [nz // 2]
    near = 5

    def slot(rel):
        return REL.index(rel if rel in REL else (rel % nz))

    y = lax.axis_index("narrow")
    ep = lax.axis_index("ep")
    z = ep // GROUP
    j = ep % GROUP
    x = j // 2
    core = j % 2

    def at(dy=0, dz=0, dx=0, flip=False):
        yy = (y + dy + ny) % ny
        zz = (z + dz + nz) % nz
        xx = (x + dx + NX) % NX
        cc = 1 - core if flip else core
        return (yy, zz * GROUP + xx * 2 + cc)

    barrier = pltpu.get_barrier_semaphore()
    partners = [at(dz=1), at(dz=-1), at(dz=2), at(dz=-2)]
    partners += [(y, z * GROUP + (j + k) % GROUP) for k in range(1, GROUP)]
    partners += [at(dy=d) for d in range(1, ny)]
    for p in partners:
        pl.semaphore_signal(barrier, inc=1, device_id=p, device_id_type=MESH)

    loads = []

    def load(src, dst):
        c = pltpu.make_async_copy(src, dst, in_sem.at[len(loads)])
        c.start()
        loads.append(c)
        return c

    def w_rows(jj):
        return w_ref.at[pl.ds(pl.multiple_of(jj * cols, 16), cols), :]

    res_load = load(res_hbm, res_ref)
    mask_loads = [load(vis_hbm, vis_ref), load(len_hbm, len_ref)]
    tree_loads = []
    for t in range(trees):
        tree_loads.append(
            [
                load(q_hbm.at[t], q_ref.at[t]),
                load(trunk_hbm.at[t], trunk_ref.at[t]),
                load(branch_hbm.at[t], branch_ref.at[t]),
            ]
        )
    vup_load = load(vup_hbm, vup_ref)
    own_w = load(w_hbm, w_rows(j))
    late_loads = [load(ids_hbm, ids_ref), load(gain_hbm, gain_ref)]

    sends = []
    ids = Ids()

    def copy(name, src, dst, dev):
        i = ids(*name)
        c = pltpu.make_async_remote_copy(
            src_ref=src,
            dst_ref=dst,
            send_sem=send_sem.at[i],
            recv_sem=recv_sem.at[i],
            device_id=dev,
            device_id_type=MESH,
        )
        c.start()
        sends.append(c)

    def arrived(name, dst):
        i = ids(*name)
        pltpu.make_async_remote_copy(
            src_ref=dst,
            dst_ref=dst,
            send_sem=send_sem.at[i],
            recv_sem=recv_sem.at[i],
            device_id=at(flip=True),
            device_id_type=MESH,
        ).wait_recv()

    pl.semaphore_wait(barrier, len(partners))

    def xj(dx):
        return ((x + dx + NX) % NX) * 2 + core

    def xj_other(dx):
        return ((x + dx + NX) % NX) * 2 + (1 - core)

    for d in (1, -1, 2):
        copy(("w", d), w_hbm, w_rows(j), at(dx=d))
    copy(("ws", 0), w_hbm, w_rows(j), at(flip=True))

    res_load.wait()
    res = res_ref[...]
    fill = 128 - cols
    if fill:
        res = jnp.concatenate([res, jnp.zeros((fill, block), bf16)], axis=0)
    ri = lax.broadcasted_iota(i32, (block, block), 0)
    ci = lax.broadcasted_iota(i32, (block, block), 1)
    eye = (ri == ci).astype(f32).astype(bf16)
    rt_ref[...] = matmul(eye, res, NT).astype(bf16).reshape(GROUP, toks, 128)
    for k in range(1, GROUP):
        jj = (j + k) % GROUP
        copy(("r", k), rt_ref.at[jj], rb_ref.at[j], (y, z * GROUP + jj))

    def z_first(name, part):
        for d in (2, 1):
            for way in (1, -1):
                copy((name, -way * d), part(0, None), part(slot(-way * d), None), at(dz=way * d))

    def z_second(name, part):
        for way in (1, -1):
            arrived((name, -2 * way), part(slot(-2 * way), None))
            src = slot(-2 * way)
            copy((name, -3 * way), part(src, None), part(slot(-3 * way), None), at(dz=way))
            copy((name, 4, way), part(src, way), part(slot(4), way), at(dz=2 * way))

    def z_near(name, part):
        for way in (1, -1):
            arrived((name, -way), part(slot(-way), None))

    def z_far(name, part):
        for way in (1, -1):
            arrived((name, -3 * way), part(slot(-3 * way), None))
            arrived((name, 4, way), part(slot(4), way))

    feat = heads * vdim

    def f_part(t):
        def part(s, way):
            c = slice(None) if way is None else slice(0, feat // 2) if way > 0 else slice(feat // 2, feat)
            return feat_ref.at[s, t * branches : (t + 1) * branches, c]

        return part

    ro = lax.broadcasted_iota(i32, (rows, rows), 0)
    co = lax.broadcasted_iota(i32, (rows, rows), 1)
    swap = (co == (ro % branches) * heads + ro // branches).astype(f32).astype(bf16)
    for c in mask_loads:
        c.wait()
    for t in range(trees):
        key_i = lax.broadcasted_iota(i32, (branches, nkeys), 1)
        owner = key_i // brmost
        pos = key_i % brmost
        vis = jnp.zeros((branches, nkeys), i32)
        lim = jnp.zeros((branches, nkeys), i32)
        for b in range(branches):
            here = owner == b
            vis = jnp.where(here, vis_ref[t, :, b : b + 1], vis)
            lim = jnp.where(here, len_ref[t : t + 1, b : b + 1], lim)
        live = (vis > 0) & (pos < lim)
        bias_ref[...] = jnp.where(live, 0.0, -1e30)

        for c in tree_loads[t]:
            c.wait()
        q = q_ref[t]
        s_ref[:, :trunk_len] = matmul(q, trunk_ref[t])
        s_ref[:, trunk_len:] = matmul(q, branch_ref[t], NT)

        def soft(b, carry):
            r = pl.ds(pl.multiple_of(b * heads, heads), heads)
            st = s_ref[r, :trunk_len] * score_scale
            sb = s_ref[r, trunk_len:] * score_scale + bias_ref[pl.ds(b, 1), :]
            top = jnp.maximum(
                jnp.max(st, axis=-1, keepdims=True), jnp.max(sb, axis=-1, keepdims=True)
            )
            et = jnp.exp(st - top)
            eb = jnp.exp(sb - top)
            inv = 1.0 / (
                jnp.sum(et, axis=-1, keepdims=True) + jnp.sum(eb, axis=-1, keepdims=True)
            )
            p_ref[r, :trunk_len] = (et * inv).astype(bf16)
            p_ref[r, trunk_len:] = (eb * inv).astype(bf16)
            return carry

        lax.fori_loop(0, branches, soft, 0, unroll=4)
        o = matmul(p_ref[:, :trunk_len], trunk_ref[t, :lat, :], NT)
        o = o + matmul(p_ref[:, trunk_len:], branch_ref[t, :, :lat])
        o = matmul(swap, o.astype(bf16)).astype(bf16)
        lat_ref[...] = o.reshape(heads, branches, lat)
        if t == 0:
            vup_load.wait()
        for h in range(heads):
            f = matmul(lat_ref[h], vup_ref[h])
            feat_ref[0, t * branches : (t + 1) * branches, h * vdim : (h + 1) * vdim] = f.astype(bf16)
        z_first("f%d" % t, f_part(t))

    for c in late_loads:
        c.wait()
    id_rows = ids_ref[...]
    marks = jnp.zeros((16, block), f32)
    mrow = lax.broadcasted_iota(i32, (16, block), 0)
    for e in range(EXP_DEV):
        hit = jnp.where(id_rows == ep * EXP_DEV + e, 1.0, 0.0)
        hit = jnp.sum(hit, axis=0, keepdims=True)
        marks = jnp.where(mrow == e, hit, marks)
    earlier = (ri < ci).astype(f32).astype(bf16)
    before = matmul(marks.astype(bf16), earlier)
    srow = lax.broadcasted_iota(i32, (SLOTS, block), 0).astype(f32)
    for e in range(EXP_DEV):
        chosen = (before[e : e + 1, :] == srow) & (marks[e : e + 1, :] > 0.5)
        onehot_ref[e * SLOTS : (e + 1) * SLOTS, :] = jnp.where(chosen, 1.0, 0.0).astype(bf16)

    z_second("f0", f_part(0))
    for d in (1, -1):
        arrived(("w", d), w_rows(xj(-d)))
        copy(("ws", d), w_rows(xj(-d)), w_rows(xj(-d)), at(flip=True))
    for t in range(1, trees):
        z_second("f%d" % t, f_part(t))

    rb_ref[j] = rt_ref[j]
    for k in range(1, GROUP):
        arrived(("r", k), rb_ref.at[(j + GROUP - k) % GROUP])
    residual = jnp.concatenate(
        [rb_ref[g].astype(f32)[:, :cols] for g in range(GROUP)], axis=1
    )
    sum_ref[...] = residual

    arrived(("w", 2), w_rows(xj(2)))
    copy(("ws", 2), w_rows(xj(2)), w_rows(xj(2)), at(flip=True))
    own_w.wait()
    for d in (0, 1, -1, 2):
        arrived(("ws", d), w_rows(xj_other(-d)))
    for t in range(trees):
        z_near("f%d" % t, f_part(t))

    p_ids = [ids("p", d) for d in range(1, ny)]
    assert p_ids[-1] - p_ids[0] == ny - 2

    def part_copy(s, d):
        return pltpu.make_async_remote_copy(
            src_ref=part16_ref.at[s],
            dst_ref=got_ref.at[d - 1],
            send_sem=send_sem.at[p_ids[0] + d - 1],
            recv_sem=recv_sem.at[p_ids[0] + d - 1],
            device_id=at(dy=d),
            device_id_type=MESH,
        )

    def project(first, last):
        feats = feat_ref[first:last].reshape((last - first) * toks, feat)
        for lo in range(0, cz, 256):
            hi = min(cz, lo + 256)
            prod = matmul(feats, w_ref[lo:hi, :], NT).reshape(last - first, toks, hi - lo)
            part_ref[first:last, :, lo:hi] = prod
            part16_ref[first:last, :, lo:hi] = prod.astype(bf16)
        for s in range(first, last):
            d = (z + REL[s] - y + 2 * ny) % ny

            @pl.when(d != 0)
            def _():
                part_copy(s, d).start()

    project(0, near)
    for t in range(trees):
        z_far("f%d" % t, f_part(t))
    project(near, nz)
    dz_own = (y - z + nz) % nz
    own_slot = jnp.maximum(
        0, 2 * jnp.minimum(dz_own, nz - dz_own) - 1 + (dz_own > nz // 2).astype(i32)
    )
    total = part_ref[own_slot]
    for d in range(1, ny):
        arrived(("p", d), got_ref.at[d - 1])
        total = total + got_ref[d - 1].astype(f32)
    hidden = (sum_ref[...] + total).astype(bf16)

    ca = max(1, (cz * 5 // 7) // 128) * 128
    h_ref[0, x, core] = hidden

    def row_half(way):
        if way is None:
            return slice(None)
        return slice(0, toks // 2) if way > 0 else slice(toks // 2, toks)

    def a1(s, way):
        return h_ref.at[s, x, core, row_half(way), :ca]

    def b2(s, way):
        return h_ref.at[s, :, core, row_half(way), ca:]

    def b1(dx):
        return h_ref.at[0, (x + dx + NX) % NX, core, :, ca:]

    parts_z = ((0, 1), (1, near), (near, nz))

    def a2(g, dx):
        return h_ref.at[parts_z[g][0] : parts_z[g][1], (x + dx + NX) % NX, core, :, :ca]

    def a2_send(g):
        for d in (2, 1, -1):
            copy(("a2", g, d), a2(g, 0), a2(g, 0), at(dx=d))

    def a2_take(g):
        for d in (1, -1, 2):
            arrived(("a2", g, d), a2(g, -d))
        s = h_ref.at[parts_z[g][0] : parts_z[g][1], :, core, :, :ca]
        copy(("as", g), s, s, at(flip=True))

    def b_share(g):
        s = h_ref.at[parts_z[g][0] : parts_z[g][1], :, core, :, ca:]
        copy(("bs", g), s, s, at(flip=True))

    def shared(g):
        c = slice(parts_z[g][0], parts_z[g][1])
        arrived(("as", g), h_ref.at[c, :, 1 - core, :, :ca])
        arrived(("bs", g), h_ref.at[c, :, 1 - core, :, ca:])

    for d in (2, 1, -1):
        copy(("b1", d), b1(0), b1(0), at(dx=d))
    z_first("a1", a1)
    a2_send(0)
    for d in (1, -1, 2):
        arrived(("b1", d), b1(-d))
    z_first("b2", b2)
    b_share(0)
    z_second("a1", a1)
    z_near("a1", a1)
    a2_send(1)
    a2_take(0)
    z_second("b2", b2)
    z_near("b2", b2)
    b_share(1)
    z_far("a1", a1)
    a2_send(2)
    a2_take(1)
    shared(0)

    si = lax.broadcasted_iota(i32, (cols, cz), 0)
    sc = lax.broadcasted_iota(i32, (cols, cz), 1)
    mine = (sc == si + j * cols).astype(f32).astype(bf16)
    hid_ref[...] = matmul(mine, h_ref[0].reshape(block, cz), NT).astype(bf16)

    def pick(g, squares):
        for s in range(*parts_z[g]):
            got = matmul(onehot_ref[...], h_ref[s].reshape(block, cz))
            picked_ref[s] = got
            squares = squares + jnp.sum(got * got, axis=-1, keepdims=True)
        return squares

    squares = pick(0, jnp.zeros((EXP_DEV * SLOTS, 1), f32))
    z_far("b2", b2)
    b_share(2)
    shared(1)
    squares = pick(1, squares)
    a2_take(2)
    shared(2)
    squares = pick(2, squares)
    scale = lax.rsqrt(squares / width + norm_eps)
    for s in range(nz):
        at_z = pl.ds(pl.multiple_of(((z + REL[s] + nz) % nz) * cz, 128), cz)
        out_ref[:, at_z] = (picked_ref[s] * scale * gain_ref[:, at_z]).astype(bf16)

    for d in range(1, ny):
        part_copy(0, d).wait_send()
    for c in sends:
        c.wait_send()
    assert len(ids.names) <= sem_count


def shards(
    queries,
    trunk_cache,
    branch_cache,
    visible,
    branch_len,
    value_up,
    out_proj,
    residual_in,
    norm_gain,
    expert_ids,
):
    ny = lax.axis_size("narrow")
    nz = lax.axis_size("ep") // GROUP
    trees, branches = branch_len.shape
    heads, lat, vdim = value_up.shape
    kdim = queries.shape[2]
    trunk_len = trunk_cache.shape[1]
    nkeys = branches * branch_cache.shape[2]
    feat, cols = out_proj.shape
    block = residual_in.shape[0]
    toks = trees * branches
    rows = branches * heads
    cz = GROUP * cols
    width = nz * cz
    bf16, f32 = jnp.bfloat16, jnp.float32
    sem_count = 96
    hbm = pl.BlockSpec(memory_space=pl.ANY)
    vmem = pl.BlockSpec(memory_space=pltpu.VMEM)
    chosen = EXP_DEV * SLOTS
    hidden, rows_out = pl.pallas_call(
        functools.partial(kernel, (ny, nz, sem_count)),
        out_shape=(
            jax.ShapeDtypeStruct((cols, block), bf16),
            jax.ShapeDtypeStruct((chosen, width), bf16),
        ),
        in_specs=[hbm] * 10,
        out_specs=(vmem, vmem),
        scratch_shapes=[
            pltpu.VMEM((trees, rows, kdim), bf16),
            pltpu.VMEM((trees, kdim, trunk_len), bf16),
            pltpu.VMEM((trees, nkeys, kdim), bf16),
            pltpu.VMEM((heads, lat, vdim), bf16),
            pltpu.VMEM(visible.shape, jnp.int32),
            pltpu.VMEM(branch_len.shape, jnp.int32),
            pltpu.VMEM((cols, block), bf16),
            pltpu.VMEM((1, width), f32),
            pltpu.VMEM(expert_ids.shape[::-1], jnp.int32),
            pltpu.VMEM((rows, trunk_len + nkeys), f32),
            pltpu.VMEM((rows, trunk_len + nkeys), bf16),
            pltpu.VMEM((branches, nkeys), f32),
            pltpu.VMEM((heads, branches, lat), bf16),
            pltpu.VMEM((nz, toks, feat), bf16),
            pltpu.VMEM((cz, feat), bf16),
            pltpu.VMEM((GROUP, toks, 128), bf16),
            pltpu.VMEM((GROUP, toks, 128), bf16),
            pltpu.VMEM((nz, toks, cz), f32),
            pltpu.VMEM((nz, toks, cz), bf16),
            pltpu.VMEM((ny - 1, toks, cz), bf16),
            pltpu.VMEM((toks, cz), f32),
            pltpu.VMEM((nz, NX, 2, toks, cz), bf16),
            pltpu.VMEM((chosen, block), bf16),
            pltpu.VMEM((nz, chosen, cz), f32),
            pltpu.SemaphoreType.DMA((16,)),
            pltpu.SemaphoreType.DMA((sem_count,)),
            pltpu.SemaphoreType.DMA((sem_count,)),
        ],
        compiler_params=pltpu.CompilerParams(
            collective_id=0, has_side_effects=True, vmem_limit_bytes=63 * 1024 * 1024
        ),
        name="decode_layer",
    )(
        queries.reshape(trees, rows, kdim),
        jnp.swapaxes(trunk_cache, 1, 2),
        branch_cache.reshape(trees, nkeys, kdim),
        value_up,
        out_proj.T,
        visible,
        branch_len,
        residual_in.T,
        norm_gain.reshape(1, width),
        expert_ids.T,
    )
    return hidden.T, rows_out.reshape(1, EXP_DEV, SLOTS, width)


def solution(mesh):
    placed = (
        P("ep", "narrow", None),
        P("ep", None, None),
        P("ep", None, None, None),
        P("ep", None, None),
        P("ep", None),
        P("narrow", None, None),
        P("narrow", "ep"),
        P("narrow", "ep"),
        P(),
        P("narrow", None),
    )
    return jax.shard_map(
        shards,
        mesh=mesh,
        in_specs=placed,
        out_specs=(P("narrow", "ep"), P("narrow", "ep", None, None)),
        check_vma=False,
    )
```

```python
import functools

import jax
import jax.numpy as jnp
from jax import lax
from jax.experimental import pallas as pl
from jax.experimental.pallas import tpu as pltpu
from jax.sharding import PartitionSpec as P

NX = 4
GROUP = 2 * NX
EXP_DEV = 4
SLOTS = 16

score_scale = 192.0 ** (-0.5)
norm_eps = 1e-06

MESH = pl.DeviceIdType.MESH
NT = (((1,), (1,)), ((), ()))
NN = (((1,), (0,)), ((), ()))


def matmul(a, b, dims=NN):
    return lax.dot_general(a, b, dims, preferred_element_type=jnp.float32)


class Ids:
    def __init__(self):
        self.names = {}

    def __call__(self, *name):
        return self.names.setdefault(name, len(self.names))


def kernel(
    cfg,
    q_hbm,
    trunk_hbm,
    branch_hbm,
    vup_hbm,
    w_hbm,
    vis_hbm,
    len_hbm,
    res_hbm,
    gain_hbm,
    ids_hbm,
    hid_ref,
    out_ref,
    q_ref,
    trunk_ref,
    branch_ref,
    vup_ref,
    vis_ref,
    len_ref,
    res_ref,
    gain_ref,
    ids_ref,
    s_ref,
    p_ref,
    bias_ref,
    lat_ref,
    feat_ref,
    w_ref,
    rt_ref,
    rb_ref,
    part_ref,
    part16_ref,
    got_ref,
    sum_ref,
    h_ref,
    onehot_ref,
    picked_ref,
    in_sem,
    send_sem,
    recv_sem,
):
    ny, nz, sem_count = cfg
    trees, rows, kdim = q_ref.shape
    trunk_len = trunk_ref.shape[2]
    nkeys = branch_ref.shape[1]
    heads, lat, vdim = vup_ref.shape
    branches = vis_ref.shape[1]
    brmost = nkeys // branches
    cols = w_hbm.shape[0]
    cz = GROUP * cols
    toks = trees * branches
    block = GROUP * toks
    width = nz * cz
    bf16, f32, i32 = jnp.bfloat16, jnp.float32, jnp.int32
    REL = [0] + [w * d for d in range(1, nz // 2) for w in (1, -1)] + [nz // 2]
    near = 5

    def slot(rel):
        return REL.index(rel if rel in REL else (rel % nz))

    y = lax.axis_index("narrow")
    ep = lax.axis_index("ep")
    z = ep // GROUP
    j = ep % GROUP
    x = j // 2
    core = j % 2

    def at(dy=0, dz=0, dx=0, flip=False):
        yy = (y + dy + ny) % ny
        zz = (z + dz + nz) % nz
        xx = (x + dx + NX) % NX
        cc = 1 - core if flip else core
        return (yy, zz * GROUP + xx * 2 + cc)

    barrier = pltpu.get_barrier_semaphore()
    partners = [at(dz=1), at(dz=-1), at(dz=2), at(dz=-2)]
    partners += [(y, z * GROUP + (j + k) % GROUP) for k in range(1, GROUP)]
    partners += [at(dy=d) for d in range(1, ny)]
    for p in partners:
        pl.semaphore_signal(barrier, inc=1, device_id=p, device_id_type=MESH)

    loads = []

    def load(src, dst):
        c = pltpu.make_async_copy(src, dst, in_sem.at[len(loads)])
        c.start()
        loads.append(c)
        return c

    def w_rows(jj, lo=0, hi=cols):
        return w_ref.at[pl.ds(pl.multiple_of(jj * cols + lo, 16), hi - lo), :]

    res_load = load(res_hbm, res_ref)
    mask_loads = [load(vis_hbm, vis_ref), load(len_hbm, len_ref)]
    tree_loads = []
    for t in range(trees):
        tree_loads.append(
            [
                load(q_hbm.at[t], q_ref.at[t]),
                load(trunk_hbm.at[t], trunk_ref.at[t]),
                load(branch_hbm.at[t], branch_ref.at[t]),
            ]
        )
    vup_load = load(vup_hbm, vup_ref)
    own_w = load(w_hbm, w_rows(j))
    late_loads = [load(ids_hbm, ids_ref), load(gain_hbm, gain_ref)]

    sends = []
    ids = Ids()

    def copy(name, src, dst, dev):
        i = ids(*name)
        c = pltpu.make_async_remote_copy(
            src_ref=src,
            dst_ref=dst,
            send_sem=send_sem.at[i],
            recv_sem=recv_sem.at[i],
            device_id=dev,
            device_id_type=MESH,
        )
        c.start()
        sends.append(c)

    def arrived(name, dst):
        i = ids(*name)
        pltpu.make_async_remote_copy(
            src_ref=dst,
            dst_ref=dst,
            send_sem=send_sem.at[i],
            recv_sem=recv_sem.at[i],
            device_id=at(flip=True),
            device_id_type=MESH,
        ).wait_recv()

    for c in mask_loads:
        c.wait()
    for t in range(trees):
        key_i = lax.broadcasted_iota(i32, (branches, nkeys), 1)
        owner = key_i // brmost
        pos = key_i % brmost
        vis = jnp.zeros((branches, nkeys), i32)
        lim = jnp.zeros((branches, nkeys), i32)
        for b in range(branches):
            here = owner == b
            vis = jnp.where(here, vis_ref[t, :, b : b + 1], vis)
            lim = jnp.where(here, len_ref[t : t + 1, b : b + 1], lim)
        live = (vis > 0) & (pos < lim)
        bias_ref[t] = jnp.where(live, 0.0, -1e30)

    pl.semaphore_wait(barrier, len(partners))

    def xj(dx):
        return ((x + dx + NX) % NX) * 2 + core

    def xj_other(dx):
        return ((x + dx + NX) % NX) * 2 + (1 - core)

    w_cut = (cols // 16 + 1) // 2 * 16

    def w_part(way, first):
        return (0, w_cut) if (way > 0) == first else (w_cut, cols)

    def w_send(way, first):
        lo, hi = w_part(way, first)
        copy(("w", way, first), w_hbm.at[lo:hi, :], w_rows(j, lo, hi), at(dx=way))

    def w_take(way, first):
        arrived(("w", way, first), w_rows(xj(-way), *w_part(way, first)))

    for way in (1, -1):
        w_send(way, True)
    copy(("ws", 0), w_hbm, w_rows(j), at(flip=True))

    res_load.wait()
    res = res_ref[...]
    fill = 128 - cols
    if fill:
        res = jnp.concatenate([res, jnp.zeros((fill, block), bf16)], axis=0)
    ri = lax.broadcasted_iota(i32, (block, block), 0)
    ci = lax.broadcasted_iota(i32, (block, block), 1)
    eye = (ri == ci).astype(f32).astype(bf16)
    rt_ref[...] = matmul(eye, res, NT).astype(bf16).reshape(GROUP, toks, 128)
    for k in range(1, GROUP):
        jj = (j + k) % GROUP
        copy(("r", k), rt_ref.at[jj], rb_ref.at[j], (y, z * GROUP + jj))
    for way in (1, -1):
        w_send(way, False)

    def z_first(name, part):
        for d in (2, 1):
            for way in (1, -1):
                copy((name, -way * d), part(0, None), part(slot(-way * d), None), at(dz=way * d))

    def z_second(name, part):
        for way in (1, -1):
            arrived((name, -2 * way), part(slot(-2 * way), None))
            src = slot(-2 * way)
            copy((name, -3 * way), part(src, None), part(slot(-3 * way), None), at(dz=way))
            copy((name, 4, way), part(src, way), part(slot(4), way), at(dz=2 * way))

    def z_near(name, part):
        for way in (1, -1):
            arrived((name, -way), part(slot(-way), None))

    def z_far(name, part):
        for way in (1, -1):
            arrived((name, -3 * way), part(slot(-3 * way), None))
            arrived((name, 4, way), part(slot(4), way))

    feat = heads * vdim

    def f_part(t):
        def part(s, way):
            c = slice(None) if way is None else slice(0, feat // 2) if way > 0 else slice(feat // 2, feat)
            return feat_ref.at[s, t * branches : (t + 1) * branches, c]

        return part

    ro = lax.broadcasted_iota(i32, (rows, rows), 0)
    co = lax.broadcasted_iota(i32, (rows, rows), 1)
    swap = (co == (ro % branches) * heads + ro // branches).astype(f32).astype(bf16)
    for t in range(trees):
        for c in tree_loads[t]:
            c.wait()
        q = q_ref[t]
        s_ref[:, :trunk_len] = matmul(q, trunk_ref[t])
        s_ref[:, trunk_len:] = matmul(q, branch_ref[t], NT)

        def soft(b, carry):
            r = pl.ds(pl.multiple_of(b * heads, heads), heads)
            st = s_ref[r, :trunk_len] * score_scale
            sb = s_ref[r, trunk_len:] * score_scale + bias_ref[t, pl.ds(b, 1), :]
            top = jnp.maximum(
                jnp.max(st, axis=-1, keepdims=True), jnp.max(sb, axis=-1, keepdims=True)
            )
            et = jnp.exp(st - top)
            eb = jnp.exp(sb - top)
            inv = 1.0 / (
                jnp.sum(et, axis=-1, keepdims=True) + jnp.sum(eb, axis=-1, keepdims=True)
            )
            p_ref[r, :trunk_len] = (et * inv).astype(bf16)
            p_ref[r, trunk_len:] = (eb * inv).astype(bf16)
            return carry

        lax.fori_loop(0, branches, soft, 0, unroll=4)
        o = matmul(p_ref[:, :trunk_len], trunk_ref[t, :lat, :], NT)
        o = o + matmul(p_ref[:, trunk_len:], branch_ref[t, :, :lat])
        o = matmul(swap, o.astype(bf16)).astype(bf16)
        lat_ref[...] = o.reshape(heads, branches, lat)
        if t == 0:
            vup_load.wait()
        for h in range(heads):
            f = matmul(lat_ref[h], vup_ref[h])
            feat_ref[0, t * branches : (t + 1) * branches, h * vdim : (h + 1) * vdim] = f.astype(bf16)
        z_first("f%d" % t, f_part(t))

    for c in late_loads:
        c.wait()
    id_rows = ids_ref[...]
    marks = jnp.zeros((16, block), f32)
    mrow = lax.broadcasted_iota(i32, (16, block), 0)
    for e in range(EXP_DEV):
        hit = jnp.where(id_rows == ep * EXP_DEV + e, 1.0, 0.0)
        hit = jnp.sum(hit, axis=0, keepdims=True)
        marks = jnp.where(mrow == e, hit, marks)
    earlier = (ri < ci).astype(f32).astype(bf16)
    before = matmul(marks.astype(bf16), earlier)
    srow = lax.broadcasted_iota(i32, (SLOTS, block), 0).astype(f32)
    for e in range(EXP_DEV):
        chosen = (before[e : e + 1, :] == srow) & (marks[e : e + 1, :] > 0.5)
        onehot_ref[e * SLOTS : (e + 1) * SLOTS, :] = jnp.where(chosen, 1.0, 0.0).astype(bf16)

    for way in (1, -1):
        w_take(way, True)
        w = w_rows(xj(-way), *w_part(way, True))
        copy(("w2", way), w, w, at(dx=way))
    z_second("f0", f_part(0))
    for way in (1, -1):
        w_take(way, False)
        w = w_rows(xj(-way))
        copy(("ws", way), w, w, at(flip=True))
    for t in range(1, trees):
        z_second("f%d" % t, f_part(t))

    rb_ref[j] = rt_ref[j]
    for k in range(1, GROUP):
        arrived(("r", k), rb_ref.at[(j + GROUP - k) % GROUP])
    residual = jnp.concatenate(
        [rb_ref[g].astype(f32)[:, :cols] for g in range(GROUP)], axis=1
    )
    sum_ref[...] = residual

    for way in (1, -1):
        w = w_rows(xj(2), *w_part(way, True))
        arrived(("w2", way), w)
        copy(("ws2", way), w, w, at(flip=True))
    own_w.wait()
    for d in (0, 1, -1):
        arrived(("ws", d), w_rows(xj_other(-d)))
    for way in (1, -1):
        arrived(("ws2", way), w_rows(xj_other(2), *w_part(way, True)))
    for t in range(trees):
        z_near("f%d" % t, f_part(t))

    ca = max(1, (cz * 5 // 7) // 128) * 128
    parts_c = (slice(0, ca), slice(ca, cz))
    p_ids = [ids("p", h, d) for h in range(2) for d in range(1, ny)]
    assert p_ids[-1] - p_ids[0] == 2 * (ny - 1) - 1

    def part_copy(s, h, d):
        i = p_ids[0] + h * (ny - 1) + d - 1
        return pltpu.make_async_remote_copy(
            src_ref=part16_ref.at[s, :, parts_c[h]],
            dst_ref=got_ref.at[d - 1, :, parts_c[h]],
            send_sem=send_sem.at[i],
            recv_sem=recv_sem.at[i],
            device_id=at(dy=d),
            device_id_type=MESH,
        )

    def project(first, last, h):
        feats = feat_ref[first:last].reshape((last - first) * toks, feat)
        for lo in range(parts_c[h].start, parts_c[h].stop, 256):
            hi = min(parts_c[h].stop, lo + 256)
            prod = matmul(feats, w_ref[lo:hi, :], NT).reshape(last - first, toks, hi - lo)
            part_ref[first:last, :, lo:hi] = prod
            part16_ref[first:last, :, lo:hi] = prod.astype(bf16)
        for s in range(first, last):
            d = (z + REL[s] - y + 2 * ny) % ny

            @pl.when(d != 0)
            def _():
                part_copy(s, h, d).start()

    dz_own = (y - z + nz) % nz
    own_slot = jnp.maximum(
        0, 2 * jnp.minimum(dz_own, nz - dz_own) - 1 + (dz_own > nz // 2).astype(i32)
    )

    def take_parts(h):
        total = part_ref[own_slot, :, parts_c[h]]
        for d in range(1, ny):
            arrived(("p", h, d), got_ref.at[d - 1, :, parts_c[h]])
            total = total + got_ref[d - 1, :, parts_c[h]].astype(f32)
        h_ref[0, x, core, :, parts_c[h]] = (sum_ref[:, parts_c[h]] + total).astype(bf16)

    project(0, near, 0)
    for t in range(trees):
        z_far("f%d" % t, f_part(t))
    project(near, nz, 0)
    project(0, near, 1)
    project(near, nz, 1)
    take_parts(0)

    def row_half(way):
        if way is None:
            return slice(None)
        return slice(0, toks // 2) if way > 0 else slice(toks // 2, toks)

    def a1(s, way):
        return h_ref.at[s, x, core, row_half(way), :ca]

    def b2(s, way):
        return h_ref.at[s, :, core, row_half(way), ca:]

    def b1(dx):
        return h_ref.at[0, (x + dx + NX) % NX, core, :, ca:]

    parts_z = ((0, 1), (1, near), (near, nz))

    def a2(g, dx):
        return h_ref.at[parts_z[g][0] : parts_z[g][1], (x + dx + NX) % NX, core, :, :ca]

    def a2_send(g):
        for d in (2, 1, -1):
            copy(("a2", g, d), a2(g, 0), a2(g, 0), at(dx=d))

    def a2_take(g):
        for d in (1, -1, 2):
            arrived(("a2", g, d), a2(g, -d))
        s = h_ref.at[parts_z[g][0] : parts_z[g][1], :, core, :, :ca]
        copy(("as", g), s, s, at(flip=True))

    def b_share(g):
        s = h_ref.at[parts_z[g][0] : parts_z[g][1], :, core, :, ca:]
        copy(("bs", g), s, s, at(flip=True))

    def shared(g):
        c = slice(parts_z[g][0], parts_z[g][1])
        arrived(("as", g), h_ref.at[c, :, 1 - core, :, :ca])
        arrived(("bs", g), h_ref.at[c, :, 1 - core, :, ca:])

    z_first("a1", a1)
    a2_send(0)
    take_parts(1)
    for d in (2, 1, -1):
        copy(("b1", d), b1(0), b1(0), at(dx=d))
    z_second("a1", a1)
    z_near("a1", a1)
    a2_send(1)
    for d in (1, -1, 2):
        arrived(("b1", d), b1(-d))
    z_first("b2", b2)
    b_share(0)
    a2_take(0)
    z_second("b2", b2)
    z_near("b2", b2)
    b_share(1)
    z_far("a1", a1)
    a2_send(2)
    a2_take(1)
    shared(0)

    si = lax.broadcasted_iota(i32, (cols, cz), 0)
    sc = lax.broadcasted_iota(i32, (cols, cz), 1)
    mine = (sc == si + j * cols).astype(f32).astype(bf16)
    hid_ref[...] = matmul(mine, h_ref[0].reshape(block, cz), NT).astype(bf16)

    def pick(g, squares):
        for s in range(*parts_z[g]):
            got = matmul(onehot_ref[...], h_ref[s].reshape(block, cz))
            picked_ref[s] = got
            squares = squares + jnp.sum(got * got, axis=-1, keepdims=True)
        return squares

    squares = pick(0, jnp.zeros((EXP_DEV * SLOTS, 1), f32))
    z_far("b2", b2)
    b_share(2)
    shared(1)
    squares = pick(1, squares)
    a2_take(2)
    shared(2)
    squares = pick(2, squares)
    scale = lax.rsqrt(squares / width + norm_eps)
    for s in range(nz):
        at_z = pl.ds(pl.multiple_of(((z + REL[s] + nz) % nz) * cz, 128), cz)
        out_ref[:, at_z] = (picked_ref[s] * scale * gain_ref[:, at_z]).astype(bf16)

    for h in range(2):
        for d in range(1, ny):
            part_copy(0, h, d).wait_send()
    for c in sends:
        c.wait_send()
    assert len(ids.names) <= sem_count


def shards(
    queries,
    trunk_cache,
    branch_cache,
    visible,
    branch_len,
    value_up,
    out_proj,
    residual_in,
    norm_gain,
    expert_ids,
):
    ny = lax.axis_size("narrow")
    nz = lax.axis_size("ep") // GROUP
    trees, branches = branch_len.shape
    heads, lat, vdim = value_up.shape
    kdim = queries.shape[2]
    trunk_len = trunk_cache.shape[1]
    nkeys = branches * branch_cache.shape[2]
    feat, cols = out_proj.shape
    block = residual_in.shape[0]
    toks = trees * branches
    rows = branches * heads
    cz = GROUP * cols
    width = nz * cz
    bf16, f32 = jnp.bfloat16, jnp.float32
    sem_count = 96
    hbm = pl.BlockSpec(memory_space=pl.ANY)
    vmem = pl.BlockSpec(memory_space=pltpu.VMEM)
    chosen = EXP_DEV * SLOTS
    hidden, rows_out = pl.pallas_call(
        functools.partial(kernel, (ny, nz, sem_count)),
        out_shape=(
            jax.ShapeDtypeStruct((cols, block), bf16),
            jax.ShapeDtypeStruct((chosen, width), bf16),
        ),
        in_specs=[hbm] * 10,
        out_specs=(vmem, vmem),
        scratch_shapes=[
            pltpu.VMEM((trees, rows, kdim), bf16),
            pltpu.VMEM((trees, kdim, trunk_len), bf16),
            pltpu.VMEM((trees, nkeys, kdim), bf16),
            pltpu.VMEM((heads, lat, vdim), bf16),
            pltpu.VMEM(visible.shape, jnp.int32),
            pltpu.VMEM(branch_len.shape, jnp.int32),
            pltpu.VMEM((cols, block), bf16),
            pltpu.VMEM((1, width), f32),
            pltpu.VMEM(expert_ids.shape[::-1], jnp.int32),
            pltpu.VMEM((rows, trunk_len + nkeys), f32),
            pltpu.VMEM((rows, trunk_len + nkeys), bf16),
            pltpu.VMEM((trees, branches, nkeys), f32),
            pltpu.VMEM((heads, branches, lat), bf16),
            pltpu.VMEM((nz, toks, feat), bf16),
            pltpu.VMEM((cz, feat), bf16),
            pltpu.VMEM((GROUP, toks, 128), bf16),
            pltpu.VMEM((GROUP, toks, 128), bf16),
            pltpu.VMEM((nz, toks, cz), f32),
            pltpu.VMEM((nz, toks, cz), bf16),
            pltpu.VMEM((ny - 1, toks, cz), bf16),
            pltpu.VMEM((toks, cz), f32),
            pltpu.VMEM((nz, NX, 2, toks, cz), bf16),
            pltpu.VMEM((chosen, block), bf16),
            pltpu.VMEM((nz, chosen, cz), f32),
            pltpu.SemaphoreType.DMA((16,)),
            pltpu.SemaphoreType.DMA((sem_count,)),
            pltpu.SemaphoreType.DMA((sem_count,)),
        ],
        compiler_params=pltpu.CompilerParams(
            collective_id=0, has_side_effects=True, vmem_limit_bytes=63 * 1024 * 1024
        ),
        name="decode_layer",
    )(
        queries.reshape(trees, rows, kdim),
        jnp.swapaxes(trunk_cache, 1, 2),
        branch_cache.reshape(trees, nkeys, kdim),
        value_up,
        out_proj.T,
        visible,
        branch_len,
        residual_in.T,
        norm_gain.reshape(1, width),
        expert_ids.T,
    )
    return hidden.T, rows_out.reshape(1, EXP_DEV, SLOTS, width)


def solution(mesh):
    placed = (
        P("ep", "narrow", None),
        P("ep", None, None),
        P("ep", None, None, None),
        P("ep", None, None),
        P("ep", None),
        P("narrow", None, None),
        P("narrow", "ep"),
        P("narrow", "ep"),
        P(),
        P("narrow", None),
    )
    return jax.shard_map(
        shards,
        mesh=mesh,
        in_specs=placed,
        out_specs=(P("narrow", "ep"), P("narrow", "ep", None, None)),
        check_vma=False,
    )
```

```python
import functools

import jax
import jax.numpy as jnp
from jax import lax
from jax.experimental import pallas as pl
from jax.experimental.pallas import tpu as pltpu
from jax.sharding import PartitionSpec as P

NX = 4
GROUP = 2 * NX
EXP_DEV = 4
SLOTS = 16

score_scale = 192.0 ** (-0.5)
norm_eps = 1e-06

MESH = pl.DeviceIdType.MESH
NT = (((1,), (1,)), ((), ()))
NN = (((1,), (0,)), ((), ()))


def matmul(a, b, dims=NN):
    return lax.dot_general(a, b, dims, preferred_element_type=jnp.float32)


class Ids:
    def __init__(self):
        self.names = {}

    def __call__(self, *name):
        return self.names.setdefault(name, len(self.names))


def kernel(
    cfg,
    q_hbm,
    trunk_hbm,
    branch_hbm,
    vup_hbm,
    w_hbm,
    vis_hbm,
    len_hbm,
    res_hbm,
    gain_hbm,
    ids_hbm,
    hid_ref,
    out_ref,
    q_ref,
    trunk_ref,
    branch_ref,
    vup_ref,
    vis_ref,
    len_ref,
    res_ref,
    gain_ref,
    ids_ref,
    s_ref,
    p_ref,
    bias_ref,
    lat_ref,
    feat_ref,
    w_ref,
    rt_ref,
    rb_ref,
    part_ref,
    part16_ref,
    got_ref,
    sum_ref,
    h_ref,
    onehot_ref,
    picked_ref,
    in_sem,
    send_sem,
    recv_sem,
):
    ny, nz, sem_count = cfg
    trees, rows, kdim = q_ref.shape
    trunk_len = trunk_ref.shape[2]
    nkeys = branch_ref.shape[1]
    heads, lat, vdim = vup_ref.shape
    branches = vis_ref.shape[1]
    brmost = nkeys // branches
    cols = w_hbm.shape[0]
    cz = GROUP * cols
    toks = trees * branches
    block = GROUP * toks
    width = nz * cz
    bf16, f32, i32 = jnp.bfloat16, jnp.float32, jnp.int32
    REL = [0] + [w * d for d in range(1, nz // 2) for w in (1, -1)] + [nz // 2]
    near = 5

    def slot(rel):
        return REL.index(rel if rel in REL else (rel % nz))

    y = lax.axis_index("narrow")
    ep = lax.axis_index("ep")
    z = ep // GROUP
    j = ep % GROUP
    x = j // 2
    core = j % 2

    def at(dy=0, dz=0, dx=0, flip=False):
        yy = (y + dy + ny) % ny
        zz = (z + dz + nz) % nz
        xx = (x + dx + NX) % NX
        cc = 1 - core if flip else core
        return (yy, zz * GROUP + xx * 2 + cc)

    barrier = pltpu.get_barrier_semaphore()
    partners = [at(dz=1), at(dz=-1), at(dz=2), at(dz=-2)]
    partners += [(y, z * GROUP + (j + k) % GROUP) for k in range(1, GROUP)]
    partners += [at(dy=d) for d in range(1, ny)]
    for p in partners:
        pl.semaphore_signal(barrier, inc=1, device_id=p, device_id_type=MESH)

    loads = []

    def load(src, dst):
        c = pltpu.make_async_copy(src, dst, in_sem.at[len(loads)])
        c.start()
        loads.append(c)
        return c

    ORDER = (0, 1, -1, 2)

    def xj(dx):
        return ORDER.index(dx) * 2 + core

    def xj_other(dx):
        return ORDER.index(dx) * 2 + 1 - core

    def w_rows(jj, k=slice(None)):
        return w_ref.at[pl.ds(pl.multiple_of(jj * cols, 16), cols), k]

    res_load = load(res_hbm, res_ref)
    mask_loads = [load(vis_hbm, vis_ref), load(len_hbm, len_ref)]
    tree_loads = []
    for t in range(trees):
        tree_loads.append(
            [
                load(q_hbm.at[t], q_ref.at[t]),
                load(trunk_hbm.at[t], trunk_ref.at[t]),
                load(branch_hbm.at[t], branch_ref.at[t]),
            ]
        )
    vup_load = load(vup_hbm, vup_ref)
    own_w = load(w_hbm, w_rows(xj(0)))
    late_loads = [load(ids_hbm, ids_ref), load(gain_hbm, gain_ref)]

    sends = []
    ids = Ids()

    def copy(name, src, dst, dev):
        i = ids(*name)
        c = pltpu.make_async_remote_copy(
            src_ref=src,
            dst_ref=dst,
            send_sem=send_sem.at[i],
            recv_sem=recv_sem.at[i],
            device_id=dev,
            device_id_type=MESH,
        )
        c.start()
        sends.append(c)

    def arrived(name, dst):
        i = ids(*name)
        pltpu.make_async_remote_copy(
            src_ref=dst,
            dst_ref=dst,
            send_sem=send_sem.at[i],
            recv_sem=recv_sem.at[i],
            device_id=at(flip=True),
            device_id_type=MESH,
        ).wait_recv()

    for c in mask_loads:
        c.wait()
    for t in range(trees):
        key_i = lax.broadcasted_iota(i32, (branches, nkeys), 1)
        owner = key_i // brmost
        pos = key_i % brmost
        vis = jnp.zeros((branches, nkeys), i32)
        lim = jnp.zeros((branches, nkeys), i32)
        for b in range(branches):
            here = owner == b
            vis = jnp.where(here, vis_ref[t, :, b : b + 1], vis)
            lim = jnp.where(here, len_ref[t : t + 1, b : b + 1], lim)
        live = (vis > 0) & (pos < lim)
        bias_ref[t] = jnp.where(live, 0.0, -1e30)

    def scores(t):
        for c in tree_loads[t]:
            c.wait()
        q = q_ref[t]
        s_ref[:, :trunk_len] = matmul(q, trunk_ref[t])
        s_ref[:, trunk_len:] = matmul(q, branch_ref[t], NT)

        def soft(b, carry):
            r = pl.ds(pl.multiple_of(b * heads, heads), heads)
            st = s_ref[r, :trunk_len] * score_scale
            sb = s_ref[r, trunk_len:] * score_scale + bias_ref[t, pl.ds(b, 1), :]
            top = jnp.maximum(
                jnp.max(st, axis=-1, keepdims=True), jnp.max(sb, axis=-1, keepdims=True)
            )
            et = jnp.exp(st - top)
            eb = jnp.exp(sb - top)
            inv = 1.0 / (
                jnp.sum(et, axis=-1, keepdims=True) + jnp.sum(eb, axis=-1, keepdims=True)
            )
            p_ref[r, :trunk_len] = (et * inv).astype(bf16)
            p_ref[r, trunk_len:] = (eb * inv).astype(bf16)
            return carry

        lax.fori_loop(0, branches, soft, 0, unroll=4)

    scores(0)
    pl.semaphore_wait(barrier, len(partners))

    k_half = heads * vdim // 2

    def w_part(way, first):
        return slice(0, k_half) if (way > 0) == first else slice(k_half, 2 * k_half)

    def w_send(way, first):
        k = w_part(way, first)
        copy(("w", way, first), w_hbm.at[:, k], w_rows(xj(-way), k), at(dx=way))

    def w_take(way, first):
        arrived(("w", way, first), w_rows(xj(-way), w_part(way, first)))

    for way in (1, -1):
        w_send(way, True)
    copy(("ws", 0), w_hbm, w_rows(xj(0)), at(flip=True))

    res_load.wait()
    res = res_ref[...]
    fill = 128 - cols
    if fill:
        res = jnp.concatenate([res, jnp.zeros((fill, block), bf16)], axis=0)
    ri = lax.broadcasted_iota(i32, (block, block), 0)
    ci = lax.broadcasted_iota(i32, (block, block), 1)
    eye = (ri == ci).astype(f32).astype(bf16)
    rt_ref[...] = matmul(eye, res, NT).astype(bf16).reshape(GROUP, toks, 128)
    for k in range(1, GROUP):
        jj = (j + k) % GROUP
        copy(("r", k), rt_ref.at[jj], rb_ref.at[j], (y, z * GROUP + jj))

    def z_first(name, part):
        for d in (2, 1):
            for way in (1, -1):
                copy((name, -way * d), part(0, None), part(slot(-way * d), None), at(dz=way * d))

    def z_second(name, part):
        for way in (1, -1):
            arrived((name, -2 * way), part(slot(-2 * way), None))
            src = slot(-2 * way)
            copy((name, -3 * way), part(src, None), part(slot(-3 * way), None), at(dz=way))
            copy((name, 4, way), part(src, way), part(slot(4), way), at(dz=2 * way))

    def z_near(name, part):
        for way in (1, -1):
            arrived((name, -way), part(slot(-way), None))

    def z_far(name, part):
        for way in (1, -1):
            arrived((name, -3 * way), part(slot(-3 * way), None))
            arrived((name, 4, way), part(slot(4), way))

    feat = heads * vdim

    def f_part(t):
        def part(s, way):
            c = slice(None) if way is None else slice(0, feat // 2) if way > 0 else slice(feat // 2, feat)
            return feat_ref.at[s, t * branches : (t + 1) * branches, c]

        return part

    ro = lax.broadcasted_iota(i32, (rows, rows), 0)
    co = lax.broadcasted_iota(i32, (rows, rows), 1)
    swap = (co == (ro % branches) * heads + ro // branches).astype(f32).astype(bf16)
    for t in range(trees):
        if t > 0:
            scores(t)
        o = matmul(p_ref[:, :trunk_len], trunk_ref[t, :lat, :], NT)
        o = o + matmul(p_ref[:, trunk_len:], branch_ref[t, :, :lat])
        o = matmul(swap, o.astype(bf16)).astype(bf16)
        lat_ref[...] = o.reshape(heads, branches, lat)
        if t == 0:
            vup_load.wait()
        for h in range(heads):
            f = matmul(lat_ref[h], vup_ref[h])
            feat_ref[0, t * branches : (t + 1) * branches, h * vdim : (h + 1) * vdim] = f.astype(bf16)
        z_first("f%d" % t, f_part(t))
        if t == 0:
            for way in (1, -1):
                w_send(way, False)

    for c in late_loads:
        c.wait()
    id_rows = ids_ref[...]
    marks = jnp.zeros((16, block), f32)
    mrow = lax.broadcasted_iota(i32, (16, block), 0)
    for e in range(EXP_DEV):
        hit = jnp.where(id_rows == ep * EXP_DEV + e, 1.0, 0.0)
        hit = jnp.sum(hit, axis=0, keepdims=True)
        marks = jnp.where(mrow == e, hit, marks)
    earlier = (ri < ci).astype(f32).astype(bf16)
    before = matmul(marks.astype(bf16), earlier)
    srow = lax.broadcasted_iota(i32, (SLOTS, block), 0).astype(f32)
    for e in range(EXP_DEV):
        chosen = (before[e : e + 1, :] == srow) & (marks[e : e + 1, :] > 0.5)
        onehot_ref[e * SLOTS : (e + 1) * SLOTS, :] = jnp.where(chosen, 1.0, 0.0).astype(bf16)

    for way in (1, -1):
        w_take(way, True)
        k = w_part(way, True)
        copy(("w2", way), w_rows(xj(-way), k), w_rows(xj(2), k), at(dx=way))
    z_second("f0", f_part(0))
    for way in (1, -1):
        w_take(way, False)
        w = w_rows(xj(-way))
        copy(("ws", way), w, w, at(flip=True))
    for t in range(1, trees):
        z_second("f%d" % t, f_part(t))

    rb_ref[j] = rt_ref[j]
    for k in range(1, GROUP):
        arrived(("r", k), rb_ref.at[(j + GROUP - k) % GROUP])
    residual = jnp.concatenate(
        [
            rb_ref[((x + d + NX) % NX) * 2 + c].astype(f32)[:, :cols]
            for d in ORDER
            for c in range(2)
        ],
        axis=1,
    )
    sum_ref[...] = residual

    own_w.wait()
    for d in (0, 1, -1):
        arrived(("ws", d), w_rows(xj_other(-d)))

    def tree_rows(t):
        return slice(t * branches, (t + 1) * branches)

    cut = cz * 3 // 4 // 128 * 128
    halves = (slice(0, cut), slice(cut, cz))
    p_ids = [ids("p", t, h, d) for t in range(trees) for h in range(2) for d in range(1, ny)]
    assert p_ids[-1] - p_ids[0] == 2 * trees * (ny - 1) - 1

    def part_copy(s, t, h, d):
        i = p_ids[0] + (2 * t + h) * (ny - 1) + d - 1
        return pltpu.make_async_remote_copy(
            src_ref=part16_ref.at[s, tree_rows(t), halves[h]],
            dst_ref=got_ref.at[d - 1, tree_rows(t), halves[h]],
            send_sem=send_sem.at[i],
            recv_sem=recv_sem.at[i],
            device_id=at(dy=d),
            device_id_type=MESH,
        )

    def project(first, last, t, h):
        feats = feat_ref[first:last, tree_rows(t), :].reshape((last - first) * branches, feat)
        for lo in range(halves[h].start, halves[h].stop, 256):
            hi = min(halves[h].stop, lo + 256)
            prod = matmul(feats, w_ref[lo:hi, :], NT).reshape(last - first, branches, hi - lo)
            part_ref[first:last, tree_rows(t), lo:hi] = prod
            part16_ref[first:last, tree_rows(t), lo:hi] = prod.astype(bf16)
        for s in range(first, last):
            d = (z + REL[s] - y + 2 * ny) % ny

            @pl.when(d != 0)
            def _():
                part_copy(s, t, h, d).start()

    dz_own = (y - z + nz) % nz
    own_slot = jnp.maximum(
        0, 2 * jnp.minimum(dz_own, nz - dz_own) - 1 + (dz_own > nz // 2).astype(i32)
    )

    def take_parts(t):
        r = tree_rows(t)
        total = part_ref[own_slot, r, :]
        for d in range(1, ny):
            for h in range(2):
                arrived(("p", t, h, d), got_ref.at[d - 1, r, halves[h]])
            total = total + got_ref[d - 1, r, :].astype(f32)
        total = sum_ref[r, :] + total
        pair = 2 * cols
        hidden = total
        for at_x in range(NX):
            places = [ORDER.index((k - at_x + 1) % NX - 1) for k in range(NX)]
            turned = jnp.concatenate([total[:, p * pair : (p + 1) * pair] for p in places], axis=1)
            hidden = jnp.where(x == at_x, turned, hidden)
        h_ref[0, x, core, r, :] = hidden.astype(bf16)

    for t in range(trees):
        z_near("f%d" % t, f_part(t))
        project(0, near, t, 0)
    for t in range(trees):
        z_far("f%d" % t, f_part(t))
        project(near, nz, t, 0)
    for way in (1, -1):
        w = w_rows(xj(2), w_part(way, True))
        arrived(("w2", way), w)
        copy(("ws2", way), w, w, at(flip=True))
    for way in (1, -1):
        arrived(("ws2", way), w_rows(xj_other(2), w_part(way, True)))
    for t in range(trees):
        project(0, nz, t, 1)
    take_parts(0)

    assert trees == 2
    ca = (cz * 3 // 7) // 128 * 128
    whole = slice(0, cz)
    low, high = slice(0, ca), slice(ca, cz)
    three = ((0, 1), (1, near), (near, nz))
    two = ((0, near), (near, nz))

    def half_cols(c, way):
        cut = c.start + ((c.stop - c.start) // 128 + 1) // 2 * 128
        return c if way is None else slice(c.start, cut) if way > 0 else slice(cut, c.stop)

    def x_at(dx):
        return (x + dx + NX) % NX

    class Region:
        def __init__(self, name, t, c, groups):
            self.name, self.r, self.c, self.groups = name, tree_rows(t), c, groups

        def own(self, s, way):
            return h_ref.at[s, x, core, self.r, half_cols(self.c, way)]

        def every_x(self, s, way):
            return h_ref.at[s, :, core, self.r, half_cols(self.c, way)]

        def one_x(self, g, dx):
            lo, hi = self.groups[g]
            return h_ref.at[lo:hi, x_at(dx), core, self.r, self.c]

        def all_x(self, g, cc):
            lo, hi = self.groups[g]
            return h_ref.at[lo:hi, :, cc, self.r, self.c]

        def x_send(self, g):
            for d in (2, 1, -1):
                copy((self.name, "x", g, d), self.one_x(g, 0), self.one_x(g, 0), at(dx=d))

        def x_take(self, g):
            for d in (1, -1, 2):
                arrived((self.name, "x", g, d), self.one_x(g, -d))

        def share(self, g):
            copy((self.name, "s", g), self.all_x(g, core), self.all_x(g, core), at(flip=True))

        def shared(self, g):
            arrived((self.name, "s", g), self.all_x(g, 1 - core))

    ra = Region("a", 0, whole, three)
    rc = Region("c", 1, low, two)
    rb = Region("b", 1, high, three)
    z_first("az", ra.own)
    ra.x_send(0)
    take_parts(1)
    rb.x_send(0)
    z_first("cz", rc.own)
    z_second("az", ra.own)
    z_near("az", ra.own)
    ra.x_send(1)
    rb.x_take(0)
    z_first("bz", rb.every_x)
    rb.share(0)
    z_second("cz", rc.own)
    z_near("cz", rc.own)
    rc.x_send(0)
    z_far("az", ra.own)
    ra.x_send(2)
    ra.x_take(0)
    ra.share(0)
    ra.x_take(1)
    ra.share(1)
    z_second("bz", rb.every_x)
    z_near("bz", rb.every_x)
    rb.share(1)
    z_far("cz", rc.own)
    rc.x_send(1)
    rc.x_take(0)
    rc.share(0)
    ra.x_take(2)
    ra.share(2)

    def pick(first, last, squares):
        for s in range(first, last):
            got = matmul(onehot_ref[...], h_ref[s].reshape(block, cz))
            picked_ref[s] = got
            squares = squares + jnp.sum(got * got, axis=-1, keepdims=True)
        return squares

    for g in range(2):
        ra.shared(g)
        rb.shared(g)
    rc.shared(0)
    squares = pick(0, near, jnp.zeros((EXP_DEV * SLOTS, 1), f32))

    si = lax.broadcasted_iota(i32, (cols, cz), 0)
    sc = lax.broadcasted_iota(i32, (cols, cz), 1)
    mine = (sc == si + j * cols).astype(f32).astype(bf16)
    hid_ref[...] = matmul(mine, h_ref[0].reshape(block, cz), NT).astype(bf16)

    rc.x_take(1)
    rc.share(1)
    z_far("bz", rb.every_x)
    rb.share(2)
    ra.shared(2)
    rc.shared(1)
    rb.shared(2)
    squares = pick(near, nz, squares)
    scale = lax.rsqrt(squares / width + norm_eps)
    for s in range(nz):
        at_z = pl.ds(pl.multiple_of(((z + REL[s] + nz) % nz) * cz, 128), cz)
        out_ref[:, at_z] = (picked_ref[s] * scale * gain_ref[:, at_z]).astype(bf16)

    for t in range(trees):
        for h in range(2):
            for d in range(1, ny):
                part_copy(0, t, h, d).wait_send()
    for c in sends:
        c.wait_send()
    assert len(ids.names) <= sem_count


def shards(
    queries,
    trunk_cache,
    branch_cache,
    visible,
    branch_len,
    value_up,
    out_proj,
    residual_in,
    norm_gain,
    expert_ids,
):
    ny = lax.axis_size("narrow")
    nz = lax.axis_size("ep") // GROUP
    trees, branches = branch_len.shape
    heads, lat, vdim = value_up.shape
    kdim = queries.shape[2]
    trunk_len = trunk_cache.shape[1]
    nkeys = branches * branch_cache.shape[2]
    feat, cols = out_proj.shape
    block = residual_in.shape[0]
    toks = trees * branches
    rows = branches * heads
    cz = GROUP * cols
    width = nz * cz
    bf16, f32 = jnp.bfloat16, jnp.float32
    sem_count = 160
    hbm = pl.BlockSpec(memory_space=pl.ANY)
    vmem = pl.BlockSpec(memory_space=pltpu.VMEM)
    chosen = EXP_DEV * SLOTS
    hidden, rows_out = pl.pallas_call(
        functools.partial(kernel, (ny, nz, sem_count)),
        out_shape=(
            jax.ShapeDtypeStruct((cols, block), bf16),
            jax.ShapeDtypeStruct((chosen, width), bf16),
        ),
        in_specs=[hbm] * 10,
        out_specs=(vmem, vmem),
        scratch_shapes=[
            pltpu.VMEM((trees, rows, kdim), bf16),
            pltpu.VMEM((trees, kdim, trunk_len), bf16),
            pltpu.VMEM((trees, nkeys, kdim), bf16),
            pltpu.VMEM((heads, lat, vdim), bf16),
            pltpu.VMEM(visible.shape, jnp.int32),
            pltpu.VMEM(branch_len.shape, jnp.int32),
            pltpu.VMEM((cols, block), bf16),
            pltpu.VMEM((1, width), f32),
            pltpu.VMEM(expert_ids.shape[::-1], jnp.int32),
            pltpu.VMEM((rows, trunk_len + nkeys), f32),
            pltpu.VMEM((rows, trunk_len + nkeys), bf16),
            pltpu.VMEM((trees, branches, nkeys), f32),
            pltpu.VMEM((heads, branches, lat), bf16),
            pltpu.VMEM((nz, toks, feat), bf16),
            pltpu.VMEM((cz, feat), bf16),
            pltpu.VMEM((GROUP, toks, 128), bf16),
            pltpu.VMEM((GROUP, toks, 128), bf16),
            pltpu.VMEM((nz, toks, cz), f32),
            pltpu.VMEM((nz, toks, cz), bf16),
            pltpu.VMEM((ny - 1, toks, cz), bf16),
            pltpu.VMEM((toks, cz), f32),
            pltpu.VMEM((nz, NX, 2, toks, cz), bf16),
            pltpu.VMEM((chosen, block), bf16),
            pltpu.VMEM((nz, chosen, cz), f32),
            pltpu.SemaphoreType.DMA((16,)),
            pltpu.SemaphoreType.DMA((sem_count,)),
            pltpu.SemaphoreType.DMA((sem_count,)),
        ],
        compiler_params=pltpu.CompilerParams(
            collective_id=0, has_side_effects=True, vmem_limit_bytes=63 * 1024 * 1024
        ),
        name="decode_layer",
    )(
        queries.reshape(trees, rows, kdim),
        jnp.swapaxes(trunk_cache, 1, 2),
        branch_cache.reshape(trees, nkeys, kdim),
        value_up,
        out_proj.T,
        visible,
        branch_len,
        residual_in.T,
        norm_gain.reshape(1, width),
        expert_ids.T,
    )
    return hidden.T, rows_out.reshape(1, EXP_DEV, SLOTS, width)


def solution(mesh):
    placed = (
        P("ep", "narrow", None),
        P("ep", None, None),
        P("ep", None, None, None),
        P("ep", None, None),
        P("ep", None),
        P("narrow", None, None),
        P("narrow", "ep"),
        P("narrow", "ep"),
        P(),
        P("narrow", None),
    )
    return jax.shard_map(
        shards,
        mesh=mesh,
        in_specs=placed,
        out_specs=(P("narrow", "ep"), P("narrow", "ep", None, None)),
        check_vma=False,
    )
```

```python
import functools

import jax
import jax.numpy as jnp
from jax import lax
from jax.experimental import pallas as pl
from jax.experimental.pallas import tpu as pltpu
from jax.sharding import PartitionSpec as P

NX = 4
GROUP = 2 * NX
EXP_DEV = 4
SLOTS = 16

score_scale = 192.0 ** (-0.5)
norm_eps = 1e-06

MESH = pl.DeviceIdType.MESH
NT = (((1,), (1,)), ((), ()))
NN = (((1,), (0,)), ((), ()))


def matmul(a, b, dims=NN):
    return lax.dot_general(a, b, dims, preferred_element_type=jnp.float32)


class Ids:
    def __init__(self):
        self.names = {}

    def __call__(self, *name):
        return self.names.setdefault(name, len(self.names))


def kernel(
    cfg,
    q_hbm,
    trunk_hbm,
    branch_hbm,
    vup_hbm,
    w_hbm,
    vis_hbm,
    len_hbm,
    res_hbm,
    gain_hbm,
    ids_hbm,
    hid_ref,
    out_ref,
    q_ref,
    trunk_ref,
    branch_ref,
    vup_ref,
    vis_ref,
    len_ref,
    res_ref,
    gain_ref,
    ids_ref,
    s_ref,
    p_ref,
    bias_ref,
    lat_ref,
    feat_ref,
    w_ref,
    rt_ref,
    rb_ref,
    part_ref,
    part16_ref,
    got_ref,
    sum_ref,
    h_ref,
    onehot_ref,
    picked_ref,
    in_sem,
    send_sem,
    recv_sem,
):
    ny, nz, sem_count = cfg
    trees, rows, kdim = q_ref.shape
    trunk_len = trunk_ref.shape[2]
    nkeys = branch_ref.shape[1]
    heads, lat, vdim = vup_ref.shape
    branches = vis_ref.shape[1]
    brmost = nkeys // branches
    cols = w_hbm.shape[0]
    cz = GROUP * cols
    toks = trees * branches
    block = GROUP * toks
    width = nz * cz
    bf16, f32, i32 = jnp.bfloat16, jnp.float32, jnp.int32
    REL = [0] + [w * d for d in range(1, nz // 2) for w in (1, -1)] + [nz // 2]
    near = 5

    def slot(rel):
        return REL.index(rel if rel in REL else (rel % nz))

    y = lax.axis_index("narrow")
    ep = lax.axis_index("ep")
    z = ep // GROUP
    j = ep % GROUP
    x = j // 2
    core = j % 2

    def at(dy=0, dz=0, dx=0, flip=False):
        yy = (y + dy + ny) % ny
        zz = (z + dz + nz) % nz
        xx = (x + dx + NX) % NX
        cc = 1 - core if flip else core
        return (yy, zz * GROUP + xx * 2 + cc)

    barrier = pltpu.get_barrier_semaphore()
    partners = [at(dz=1), at(dz=-1), at(dz=2), at(dz=-2)]
    partners += [(y, z * GROUP + (j + k) % GROUP) for k in range(1, GROUP)]
    partners += [at(dy=d) for d in range(1, ny)]
    for p in partners:
        pl.semaphore_signal(barrier, inc=1, device_id=p, device_id_type=MESH)

    loads = []

    def load(src, dst):
        c = pltpu.make_async_copy(src, dst, in_sem.at[len(loads)])
        c.start()
        loads.append(c)
        return c

    ORDER = (0, 1, -1, 2)

    def xj(dx):
        return ORDER.index(dx) * 2 + core

    def xj_other(dx):
        return ORDER.index(dx) * 2 + 1 - core

    def w_rows(jj, k=slice(None)):
        return w_ref.at[pl.ds(pl.multiple_of(jj * cols, 16), cols), k]

    res_load = load(res_hbm, res_ref)
    mask_loads = [load(vis_hbm, vis_ref), load(len_hbm, len_ref)]
    tree_loads = []
    for t in range(trees):
        tree_loads.append(
            [
                load(q_hbm.at[t], q_ref.at[t]),
                load(trunk_hbm.at[t], trunk_ref.at[t]),
                load(branch_hbm.at[t], branch_ref.at[t]),
            ]
        )
    vup_load = load(vup_hbm, vup_ref)
    own_w = load(w_hbm, w_rows(xj(0)))
    late_loads = [load(ids_hbm, ids_ref), load(gain_hbm, gain_ref)]

    sends = []
    ids = Ids()

    def copy(name, src, dst, dev):
        i = ids(*name)
        c = pltpu.make_async_remote_copy(
            src_ref=src,
            dst_ref=dst,
            send_sem=send_sem.at[i],
            recv_sem=recv_sem.at[i],
            device_id=dev,
            device_id_type=MESH,
        )
        c.start()
        sends.append(c)

    def arrived(name, dst):
        i = ids(*name)
        pltpu.make_async_remote_copy(
            src_ref=dst,
            dst_ref=dst,
            send_sem=send_sem.at[i],
            recv_sem=recv_sem.at[i],
            device_id=at(flip=True),
            device_id_type=MESH,
        ).wait_recv()

    for c in mask_loads:
        c.wait()
    for t in range(trees):
        key_i = lax.broadcasted_iota(i32, (branches, nkeys), 1)
        owner = key_i // brmost
        pos = key_i % brmost
        vis = jnp.zeros((branches, nkeys), i32)
        lim = jnp.zeros((branches, nkeys), i32)
        for b in range(branches):
            here = owner == b
            vis = jnp.where(here, vis_ref[t, :, b : b + 1], vis)
            lim = jnp.where(here, len_ref[t : t + 1, b : b + 1], lim)
        live = (vis > 0) & (pos < lim)
        bias_ref[t] = jnp.where(live, 0.0, -1e30)

    def scores(t):
        for c in tree_loads[t]:
            c.wait()
        q = q_ref[t]
        s_ref[:, :trunk_len] = matmul(q, trunk_ref[t])
        s_ref[:, trunk_len:] = matmul(q, branch_ref[t], NT)

        def soft(b, carry):
            r = pl.ds(pl.multiple_of(b * heads, heads), heads)
            st = s_ref[r, :trunk_len] * score_scale
            sb = s_ref[r, trunk_len:] * score_scale + bias_ref[t, pl.ds(b, 1), :]
            top = jnp.maximum(
                jnp.max(st, axis=-1, keepdims=True), jnp.max(sb, axis=-1, keepdims=True)
            )
            et = jnp.exp(st - top)
            eb = jnp.exp(sb - top)
            inv = 1.0 / (
                jnp.sum(et, axis=-1, keepdims=True) + jnp.sum(eb, axis=-1, keepdims=True)
            )
            p_ref[r, :trunk_len] = (et * inv).astype(bf16)
            p_ref[r, trunk_len:] = (eb * inv).astype(bf16)
            return carry

        lax.fori_loop(0, branches, soft, 0, unroll=4)

    scores(0)
    pl.semaphore_wait(barrier, len(partners))

    k_half = heads * vdim // 2

    def w_part(way, first):
        return slice(0, k_half) if (way > 0) == first else slice(k_half, 2 * k_half)

    def w_send(way, first):
        k = w_part(way, first)
        copy(("w", way, first), w_hbm.at[:, k], w_rows(xj(-way), k), at(dx=way))

    def w_take(way, first):
        arrived(("w", way, first), w_rows(xj(-way), w_part(way, first)))

    for way in (1, -1):
        w_send(way, True)
    copy(("ws", 0), w_hbm, w_rows(xj(0)), at(flip=True))

    res_load.wait()
    res = res_ref[...]
    fill = 128 - cols
    if fill:
        res = jnp.concatenate([res, jnp.zeros((fill, block), bf16)], axis=0)
    ri = lax.broadcasted_iota(i32, (block, block), 0)
    ci = lax.broadcasted_iota(i32, (block, block), 1)
    eye = (ri == ci).astype(f32).astype(bf16)
    rt_ref[...] = matmul(eye, res, NT).astype(bf16).reshape(GROUP, toks, 128)
    for k in range(1, GROUP):
        jj = (j + k) % GROUP
        copy(("r", k), rt_ref.at[jj], rb_ref.at[j], (y, z * GROUP + jj))

    def z_first(name, part):
        for d in (2, 1):
            for way in (1, -1):
                copy((name, -way * d), part(0, None), part(slot(-way * d), None), at(dz=way * d))

    def z_second(name, part):
        for way in (1, -1):
            arrived((name, -2 * way), part(slot(-2 * way), None))
            src = slot(-2 * way)
            copy((name, -3 * way), part(src, None), part(slot(-3 * way), None), at(dz=way))
            copy((name, 4, way), part(src, way), part(slot(4), way), at(dz=2 * way))

    def z_near(name, part):
        for way in (1, -1):
            arrived((name, -way), part(slot(-way), None))

    def z_far(name, part):
        for way in (1, -1):
            arrived((name, -3 * way), part(slot(-3 * way), None))
            arrived((name, 4, way), part(slot(4), way))

    feat = heads * vdim

    def f_part(t):
        def part(s, way):
            c = slice(None) if way is None else slice(0, feat // 2) if way > 0 else slice(feat // 2, feat)
            return feat_ref.at[s, t * branches : (t + 1) * branches, c]

        return part

    ro = lax.broadcasted_iota(i32, (rows, rows), 0)
    co = lax.broadcasted_iota(i32, (rows, rows), 1)
    swap = (co == (ro % branches) * heads + ro // branches).astype(f32).astype(bf16)
    for t in range(trees):
        if t > 0:
            scores(t)
        o = matmul(p_ref[:, :trunk_len], trunk_ref[t, :lat, :], NT)
        o = o + matmul(p_ref[:, trunk_len:], branch_ref[t, :, :lat])
        o = matmul(swap, o.astype(bf16)).astype(bf16)
        lat_ref[...] = o.reshape(heads, branches, lat)
        if t == 0:
            vup_load.wait()
        for h in range(heads):
            f = matmul(lat_ref[h], vup_ref[h])
            feat_ref[0, t * branches : (t + 1) * branches, h * vdim : (h + 1) * vdim] = f.astype(bf16)
        z_first("f%d" % t, f_part(t))
        if t == 0:
            for way in (1, -1):
                w_send(way, False)

    for c in late_loads:
        c.wait()
    id_rows = ids_ref[...]
    marks = jnp.zeros((16, block), f32)
    mrow = lax.broadcasted_iota(i32, (16, block), 0)
    for e in range(EXP_DEV):
        hit = jnp.where(id_rows == ep * EXP_DEV + e, 1.0, 0.0)
        hit = jnp.sum(hit, axis=0, keepdims=True)
        marks = jnp.where(mrow == e, hit, marks)
    earlier = (ri < ci).astype(f32).astype(bf16)
    before = matmul(marks.astype(bf16), earlier)
    srow = lax.broadcasted_iota(i32, (SLOTS, block), 0).astype(f32)
    for e in range(EXP_DEV):
        chosen = (before[e : e + 1, :] == srow) & (marks[e : e + 1, :] > 0.5)
        onehot_ref[e * SLOTS : (e + 1) * SLOTS, :] = jnp.where(chosen, 1.0, 0.0).astype(bf16)

    for way in (1, -1):
        w_take(way, True)
        k = w_part(way, True)
        copy(("w2", way), w_rows(xj(-way), k), w_rows(xj(2), k), at(dx=way))
    z_second("f0", f_part(0))
    for way in (1, -1):
        w_take(way, False)
        w = w_rows(xj(-way))
        copy(("ws", way), w, w, at(flip=True))
    for t in range(1, trees):
        z_second("f%d" % t, f_part(t))

    rb_ref[j] = rt_ref[j]
    for k in range(1, GROUP):
        arrived(("r", k), rb_ref.at[(j + GROUP - k) % GROUP])
    residual = jnp.concatenate(
        [
            rb_ref[((x + d + NX) % NX) * 2 + c].astype(f32)[:, :cols]
            for d in ORDER
            for c in range(2)
        ],
        axis=1,
    )
    sum_ref[...] = residual

    own_w.wait()
    for d in (0, 1, -1):
        arrived(("ws", d), w_rows(xj_other(-d)))

    def tree_rows(t):
        return slice(t * branches, (t + 1) * branches)

    cut = cz * 3 // 4 // 128 * 128
    halves = (slice(0, cut), slice(cut, cz))
    p_ids = [ids("p", t, h, d) for t in range(trees) for h in range(2) for d in range(1, ny)]
    assert p_ids[-1] - p_ids[0] == 2 * trees * (ny - 1) - 1

    def part_copy(s, t, h, d):
        i = p_ids[0] + (2 * t + h) * (ny - 1) + d - 1
        return pltpu.make_async_remote_copy(
            src_ref=part16_ref.at[s, tree_rows(t), halves[h]],
            dst_ref=got_ref.at[d - 1, tree_rows(t), halves[h]],
            send_sem=send_sem.at[i],
            recv_sem=recv_sem.at[i],
            device_id=at(dy=d),
            device_id_type=MESH,
        )

    def project(first, last, t, h):
        feats = feat_ref[first:last, tree_rows(t), :].reshape((last - first) * branches, feat)
        for lo in range(halves[h].start, halves[h].stop, 256):
            hi = min(halves[h].stop, lo + 256)
            prod = matmul(feats, w_ref[lo:hi, :], NT).reshape(last - first, branches, hi - lo)
            part_ref[first:last, tree_rows(t), lo:hi] = prod
            part16_ref[first:last, tree_rows(t), lo:hi] = prod.astype(bf16)
        for s in range(first, last):
            d = (z + REL[s] - y + 2 * ny) % ny

            @pl.when(d != 0)
            def _():
                part_copy(s, t, h, d).start()

    dz_own = (y - z + nz) % nz
    own_slot = jnp.maximum(
        0, 2 * jnp.minimum(dz_own, nz - dz_own) - 1 + (dz_own > nz // 2).astype(i32)
    )

    def take_parts(t):
        r = tree_rows(t)
        total = part_ref[own_slot, r, :]
        for d in range(1, ny):
            for h in range(2):
                arrived(("p", t, h, d), got_ref.at[d - 1, r, halves[h]])
            total = total + got_ref[d - 1, r, :].astype(f32)
        total = sum_ref[r, :] + total
        pair = 2 * cols
        hidden = total
        for at_x in range(NX):
            places = [ORDER.index((k - at_x + 1) % NX - 1) for k in range(NX)]
            turned = jnp.concatenate([total[:, p * pair : (p + 1) * pair] for p in places], axis=1)
            hidden = jnp.where(x == at_x, turned, hidden)
        h_ref[0, x, core, r, :] = hidden.astype(bf16)

    for t in range(trees):
        z_near("f%d" % t, f_part(t))
        project(0, near, t, 0)
    for t in range(trees):
        z_far("f%d" % t, f_part(t))
        project(near, nz, t, 0)
    for way in (1, -1):
        w = w_rows(xj(2), w_part(way, True))
        arrived(("w2", way), w)
        copy(("ws2", way), w, w, at(flip=True))
    for way in (1, -1):
        arrived(("ws2", way), w_rows(xj_other(2), w_part(way, True)))
    for t in range(trees):
        project(0, nz, t, 1)
    take_parts(0)

    assert trees == 2
    ca = (cz * 2 // 7) // 128 * 128
    whole = slice(0, cz)
    low, high = slice(0, ca), slice(ca, cz)
    three = ((0, 1), (1, near), (near, nz))
    two = ((0, near), (near, nz))

    def half_cols(c, way):
        cut = c.start + ((c.stop - c.start) // 128 + 1) // 2 * 128
        return c if way is None else slice(c.start, cut) if way > 0 else slice(cut, c.stop)

    def x_at(dx):
        return (x + dx + NX) % NX

    class Region:
        def __init__(self, name, t, c, groups):
            self.name, self.r, self.c, self.groups = name, tree_rows(t), c, groups

        def own(self, s, way):
            return h_ref.at[s, x, core, self.r, half_cols(self.c, way)]

        def every_x(self, s, way):
            return h_ref.at[s, :, core, self.r, half_cols(self.c, way)]

        def one_x(self, g, dx):
            lo, hi = self.groups[g]
            return h_ref.at[lo:hi, x_at(dx), core, self.r, self.c]

        def all_x(self, g, cc):
            lo, hi = self.groups[g]
            return h_ref.at[lo:hi, :, cc, self.r, self.c]

        def x_send(self, g):
            for d in (2, 1, -1):
                copy((self.name, "x", g, d), self.one_x(g, 0), self.one_x(g, 0), at(dx=d))

        def x_take(self, g):
            for d in (1, -1, 2):
                arrived((self.name, "x", g, d), self.one_x(g, -d))

        def share(self, g):
            copy((self.name, "s", g), self.all_x(g, core), self.all_x(g, core), at(flip=True))

        def shared(self, g):
            arrived((self.name, "s", g), self.all_x(g, 1 - core))

    ra = Region("a", 0, whole, three)
    rc = Region("c", 1, low, two)
    rb = Region("b", 1, high, three)
    z_first("az", ra.own)
    ra.x_send(0)
    take_parts(1)
    rb.x_send(0)
    z_first("cz", rc.own)
    z_second("az", ra.own)
    z_near("az", ra.own)
    ra.x_send(1)
    rb.x_take(0)
    z_first("bz", rb.every_x)
    rb.share(0)
    z_second("cz", rc.own)
    z_near("cz", rc.own)
    rc.x_send(0)
    z_far("az", ra.own)
    ra.x_send(2)
    ra.x_take(0)
    ra.share(0)
    ra.x_take(1)
    ra.share(1)
    z_second("bz", rb.every_x)
    z_near("bz", rb.every_x)
    rb.share(1)
    z_far("cz", rc.own)
    rc.x_send(1)
    rc.x_take(0)
    rc.share(0)
    ra.x_take(2)
    ra.share(2)

    def pick(first, last, squares):
        for s in range(first, last):
            got = matmul(onehot_ref[...], h_ref[s].reshape(block, cz))
            picked_ref[s] = got
            squares = squares + jnp.sum(got * got, axis=-1, keepdims=True)
        return squares

    for g in range(2):
        ra.shared(g)
        rb.shared(g)
    rc.shared(0)
    squares = pick(0, near, jnp.zeros((EXP_DEV * SLOTS, 1), f32))

    si = lax.broadcasted_iota(i32, (cols, cz), 0)
    sc = lax.broadcasted_iota(i32, (cols, cz), 1)
    mine = (sc == si + j * cols).astype(f32).astype(bf16)
    hid_ref[...] = matmul(mine, h_ref[0].reshape(block, cz), NT).astype(bf16)

    rc.x_take(1)
    rc.share(1)
    z_far("bz", rb.every_x)
    rb.share(2)
    ra.shared(2)
    rc.shared(1)
    rb.shared(2)
    squares = pick(near, nz, squares)
    scale = lax.rsqrt(squares / width + norm_eps)
    for s in range(nz):
        at_z = pl.ds(pl.multiple_of(((z + REL[s] + nz) % nz) * cz, 128), cz)
        out_ref[:, at_z] = (picked_ref[s] * scale * gain_ref[:, at_z]).astype(bf16)

    for t in range(trees):
        for h in range(2):
            for d in range(1, ny):
                part_copy(0, t, h, d).wait_send()
    for c in sends:
        c.wait_send()
    assert len(ids.names) <= sem_count


def hand_over(hid_in, rows_in, hid_out, rows_out, hid_ref, rows_ref, in_sem, out_sem):
    pieces = rows_in.shape[0] // SLOTS
    moves = []
    for i in range(pieces):
        r = slice(i * SLOTS, (i + 1) * SLOTS)
        moves.append((rows_in.at[r], rows_ref.at[r], rows_out.at[r]))
    moves.append((hid_in, hid_ref, hid_out))
    ins = [pltpu.make_async_copy(m[0], m[1], in_sem.at[i]) for i, m in enumerate(moves)]
    outs = [pltpu.make_async_copy(m[1], m[2], out_sem.at[i]) for i, m in enumerate(moves)]
    for c in ins:
        c.start()
    for c, o in zip(ins, outs):
        c.wait()
        o.start()
    for o in outs:
        o.wait()


def shards(
    queries,
    trunk_cache,
    branch_cache,
    visible,
    branch_len,
    value_up,
    out_proj,
    residual_in,
    norm_gain,
    expert_ids,
):
    ny = lax.axis_size("narrow")
    nz = lax.axis_size("ep") // GROUP
    trees, branches = branch_len.shape
    heads, lat, vdim = value_up.shape
    kdim = queries.shape[2]
    trunk_len = trunk_cache.shape[1]
    nkeys = branches * branch_cache.shape[2]
    feat, cols = out_proj.shape
    block = residual_in.shape[0]
    toks = trees * branches
    rows = branches * heads
    cz = GROUP * cols
    width = nz * cz
    bf16, f32 = jnp.bfloat16, jnp.float32
    sem_count = 160
    hbm = pl.BlockSpec(memory_space=pl.ANY)
    vmem = pl.BlockSpec(memory_space=pltpu.VMEM)
    chosen = EXP_DEV * SLOTS
    hidden, rows_out = pl.pallas_call(
        functools.partial(kernel, (ny, nz, sem_count)),
        out_shape=(
            jax.ShapeDtypeStruct((cols, block), bf16),
            jax.ShapeDtypeStruct((chosen, width), bf16),
        ),
        in_specs=[hbm] * 10,
        out_specs=(vmem, vmem),
        scratch_shapes=[
            pltpu.VMEM((trees, rows, kdim), bf16),
            pltpu.VMEM((trees, kdim, trunk_len), bf16),
            pltpu.VMEM((trees, nkeys, kdim), bf16),
            pltpu.VMEM((heads, lat, vdim), bf16),
            pltpu.VMEM(visible.shape, jnp.int32),
            pltpu.VMEM(branch_len.shape, jnp.int32),
            pltpu.VMEM((cols, block), bf16),
            pltpu.VMEM((1, width), f32),
            pltpu.VMEM(expert_ids.shape[::-1], jnp.int32),
            pltpu.VMEM((rows, trunk_len + nkeys), f32),
            pltpu.VMEM((rows, trunk_len + nkeys), bf16),
            pltpu.VMEM((trees, branches, nkeys), f32),
            pltpu.VMEM((heads, branches, lat), bf16),
            pltpu.VMEM((nz, toks, feat), bf16),
            pltpu.VMEM((cz, feat), bf16),
            pltpu.VMEM((GROUP, toks, 128), bf16),
            pltpu.VMEM((GROUP, toks, 128), bf16),
            pltpu.VMEM((nz, toks, cz), f32),
            pltpu.VMEM((nz, toks, cz), bf16),
            pltpu.VMEM((ny - 1, toks, cz), bf16),
            pltpu.VMEM((toks, cz), f32),
            pltpu.VMEM((nz, NX, 2, toks, cz), bf16),
            pltpu.VMEM((chosen, block), bf16),
            pltpu.VMEM((nz, chosen, cz), f32),
            pltpu.SemaphoreType.DMA((16,)),
            pltpu.SemaphoreType.DMA((sem_count,)),
            pltpu.SemaphoreType.DMA((sem_count,)),
        ],
        compiler_params=pltpu.CompilerParams(
            collective_id=0, has_side_effects=True, vmem_limit_bytes=63 * 1024 * 1024
        ),
        name="decode_layer",
    )(
        queries.reshape(trees, rows, kdim),
        jnp.swapaxes(trunk_cache, 1, 2),
        branch_cache.reshape(trees, nkeys, kdim),
        value_up,
        out_proj.T,
        visible,
        branch_len,
        residual_in.T,
        norm_gain.reshape(1, width),
        expert_ids.T,
    )
    hidden, rows_out = pl.pallas_call(
        hand_over,
        out_shape=(
            jax.ShapeDtypeStruct(hidden.shape, bf16),
            jax.ShapeDtypeStruct(rows_out.shape, bf16),
        ),
        in_specs=[hbm] * 2,
        out_specs=(hbm, hbm),
        scratch_shapes=[
            pltpu.VMEM(hidden.shape, bf16),
            pltpu.VMEM(rows_out.shape, bf16),
            pltpu.SemaphoreType.DMA((EXP_DEV + 1,)),
            pltpu.SemaphoreType.DMA((EXP_DEV + 1,)),
        ],
        compiler_params=pltpu.CompilerParams(vmem_limit_bytes=63 * 1024 * 1024),
        name="hand_over",
    )(hidden, rows_out)
    return hidden.T, rows_out.reshape(1, EXP_DEV, SLOTS, width)


def solution(mesh):
    placed = (
        P("ep", "narrow", None),
        P("ep", None, None),
        P("ep", None, None, None),
        P("ep", None, None),
        P("ep", None),
        P("narrow", None, None),
        P("narrow", "ep"),
        P("narrow", "ep"),
        P(),
        P("narrow", None),
    )
    return jax.shard_map(
        shards,
        mesh=mesh,
        in_specs=placed,
        out_specs=(P("narrow", "ep"), P("narrow", "ep", None, None)),
        check_vma=False,
    )
```

```python
import functools

import jax
import jax.numpy as jnp
from jax import lax
from jax.experimental import pallas as pl
from jax.experimental.pallas import tpu as pltpu
from jax.sharding import PartitionSpec as P

NX = 4
GROUP = 2 * NX
EXP_DEV = 4
SLOTS = 16

score_scale = 192.0 ** (-0.5)
norm_eps = 1e-06

MESH = pl.DeviceIdType.MESH
NT = (((1,), (1,)), ((), ()))
NN = (((1,), (0,)), ((), ()))


def matmul(a, b, dims=NN):
    return lax.dot_general(a, b, dims, preferred_element_type=jnp.float32)


class Ids:
    def __init__(self):
        self.names = {}

    def __call__(self, *name):
        return self.names.setdefault(name, len(self.names))


def kernel(
    cfg,
    q_hbm,
    trunk_hbm,
    branch_hbm,
    vup_hbm,
    w_hbm,
    vis_hbm,
    len_hbm,
    res_hbm,
    gain_hbm,
    ids_hbm,
    hid_hbm,
    out_hbm,
    q_ref,
    trunk_ref,
    branch_ref,
    vup_ref,
    vis_ref,
    len_ref,
    res_ref,
    gain_ref,
    ids_ref,
    s_ref,
    p_ref,
    bias_ref,
    lat_ref,
    feat_ref,
    w_ref,
    rt_ref,
    rb_ref,
    part_ref,
    part16_ref,
    got_ref,
    sum_ref,
    h_ref,
    onehot_ref,
    picked_ref,
    hid_ref,
    out_ref,
    out_sem,
    in_sem,
    send_sem,
    recv_sem,
):
    ny, nz, sem_count = cfg
    trees, rows, kdim = q_ref.shape
    trunk_len = trunk_ref.shape[2]
    nkeys = branch_ref.shape[1]
    heads, lat, vdim = vup_ref.shape
    branches = vis_ref.shape[1]
    brmost = nkeys // branches
    cols = w_hbm.shape[0]
    cz = GROUP * cols
    toks = trees * branches
    block = GROUP * toks
    width = nz * cz
    bf16, f32, i32 = jnp.bfloat16, jnp.float32, jnp.int32
    REL = [0] + [w * d for d in range(1, nz // 2) for w in (1, -1)] + [nz // 2]
    near = 5

    def slot(rel):
        return REL.index(rel if rel in REL else (rel % nz))

    y = lax.axis_index("narrow")
    ep = lax.axis_index("ep")
    z = ep // GROUP
    j = ep % GROUP
    x = j // 2
    core = j % 2

    def at(dy=0, dz=0, dx=0, flip=False):
        yy = (y + dy + ny) % ny
        zz = (z + dz + nz) % nz
        xx = (x + dx + NX) % NX
        cc = 1 - core if flip else core
        return (yy, zz * GROUP + xx * 2 + cc)

    barrier = pltpu.get_barrier_semaphore()
    partners = [at(dz=1), at(dz=-1), at(dz=2), at(dz=-2)]
    partners += [(y, z * GROUP + (j + k) % GROUP) for k in range(1, GROUP)]
    partners += [at(dy=d) for d in range(1, ny)]
    for p in partners:
        pl.semaphore_signal(barrier, inc=1, device_id=p, device_id_type=MESH)

    loads = []

    def load(src, dst):
        c = pltpu.make_async_copy(src, dst, in_sem.at[len(loads)])
        c.start()
        loads.append(c)
        return c

    ORDER = (0, 1, -1, 2)

    def xj(dx):
        return ORDER.index(dx) * 2 + core

    def xj_other(dx):
        return ORDER.index(dx) * 2 + 1 - core

    def w_rows(jj, k=slice(None)):
        return w_ref.at[pl.ds(pl.multiple_of(jj * cols, 16), cols), k]

    res_load = load(res_hbm, res_ref)
    mask_loads = [load(vis_hbm, vis_ref), load(len_hbm, len_ref)]
    tree_loads = []
    for t in range(trees):
        tree_loads.append(
            [
                load(q_hbm.at[t], q_ref.at[t]),
                load(trunk_hbm.at[t], trunk_ref.at[t]),
                load(branch_hbm.at[t], branch_ref.at[t]),
            ]
        )
    vup_load = load(vup_hbm, vup_ref)
    own_w = load(w_hbm, w_rows(xj(0)))
    late_loads = [load(ids_hbm, ids_ref), load(gain_hbm, gain_ref)]

    sends = []
    ids = Ids()

    def copy(name, src, dst, dev):
        i = ids(*name)
        c = pltpu.make_async_remote_copy(
            src_ref=src,
            dst_ref=dst,
            send_sem=send_sem.at[i],
            recv_sem=recv_sem.at[i],
            device_id=dev,
            device_id_type=MESH,
        )
        c.start()
        sends.append(c)

    def arrived(name, dst):
        i = ids(*name)
        pltpu.make_async_remote_copy(
            src_ref=dst,
            dst_ref=dst,
            send_sem=send_sem.at[i],
            recv_sem=recv_sem.at[i],
            device_id=at(flip=True),
            device_id_type=MESH,
        ).wait_recv()

    for c in mask_loads:
        c.wait()
    for t in range(trees):
        key_i = lax.broadcasted_iota(i32, (branches, nkeys), 1)
        owner = key_i // brmost
        pos = key_i % brmost
        vis = jnp.zeros((branches, nkeys), i32)
        lim = jnp.zeros((branches, nkeys), i32)
        for b in range(branches):
            here = owner == b
            vis = jnp.where(here, vis_ref[t, :, b : b + 1], vis)
            lim = jnp.where(here, len_ref[t : t + 1, b : b + 1], lim)
        live = (vis > 0) & (pos < lim)
        bias_ref[t] = jnp.where(live, 0.0, -1e30)

    def scores(t):
        for c in tree_loads[t]:
            c.wait()
        q = q_ref[t]
        s_ref[:, :trunk_len] = matmul(q, trunk_ref[t])
        s_ref[:, trunk_len:] = matmul(q, branch_ref[t], NT)

        def soft(b, carry):
            r = pl.ds(pl.multiple_of(b * heads, heads), heads)
            st = s_ref[r, :trunk_len] * score_scale
            sb = s_ref[r, trunk_len:] * score_scale + bias_ref[t, pl.ds(b, 1), :]
            top = jnp.maximum(
                jnp.max(st, axis=-1, keepdims=True), jnp.max(sb, axis=-1, keepdims=True)
            )
            et = jnp.exp(st - top)
            eb = jnp.exp(sb - top)
            inv = 1.0 / (
                jnp.sum(et, axis=-1, keepdims=True) + jnp.sum(eb, axis=-1, keepdims=True)
            )
            p_ref[r, :trunk_len] = (et * inv).astype(bf16)
            p_ref[r, trunk_len:] = (eb * inv).astype(bf16)
            return carry

        lax.fori_loop(0, branches, soft, 0, unroll=4)

    scores(0)
    pl.semaphore_wait(barrier, len(partners))

    k_half = heads * vdim // 2

    def w_part(way, first):
        return slice(0, k_half) if (way > 0) == first else slice(k_half, 2 * k_half)

    def w_send(way, first):
        k = w_part(way, first)
        copy(("w", way, first), w_hbm.at[:, k], w_rows(xj(-way), k), at(dx=way))

    def w_take(way, first):
        arrived(("w", way, first), w_rows(xj(-way), w_part(way, first)))

    for way in (1, -1):
        w_send(way, True)
    copy(("ws", 0), w_hbm, w_rows(xj(0)), at(flip=True))

    res_load.wait()
    res = res_ref[...]
    fill = 128 - cols
    if fill:
        res = jnp.concatenate([res, jnp.zeros((fill, block), bf16)], axis=0)
    ri = lax.broadcasted_iota(i32, (block, block), 0)
    ci = lax.broadcasted_iota(i32, (block, block), 1)
    eye = (ri == ci).astype(f32).astype(bf16)
    rt_ref[...] = matmul(eye, res, NT).astype(bf16).reshape(GROUP, toks, 128)
    for k in range(1, GROUP):
        jj = (j + k) % GROUP
        copy(("r", k), rt_ref.at[jj], rb_ref.at[j], (y, z * GROUP + jj))

    def z_first(name, part):
        for d in (2, 1):
            for way in (1, -1):
                copy((name, -way * d), part(0, None), part(slot(-way * d), None), at(dz=way * d))

    def z_second(name, part):
        for way in (1, -1):
            arrived((name, -2 * way), part(slot(-2 * way), None))
            src = slot(-2 * way)
            copy((name, -3 * way), part(src, None), part(slot(-3 * way), None), at(dz=way))
            copy((name, 4, way), part(src, way), part(slot(4), way), at(dz=2 * way))

    def z_near(name, part):
        for way in (1, -1):
            arrived((name, -way), part(slot(-way), None))

    def z_far(name, part):
        for way in (1, -1):
            arrived((name, -3 * way), part(slot(-3 * way), None))
            arrived((name, 4, way), part(slot(4), way))

    feat = heads * vdim

    def f_part(t):
        def part(s, way):
            c = slice(None) if way is None else slice(0, feat // 2) if way > 0 else slice(feat // 2, feat)
            return feat_ref.at[s, t * branches : (t + 1) * branches, c]

        return part

    ro = lax.broadcasted_iota(i32, (rows, rows), 0)
    co = lax.broadcasted_iota(i32, (rows, rows), 1)
    swap = (co == (ro % branches) * heads + ro // branches).astype(f32).astype(bf16)
    for t in range(trees):
        if t > 0:
            scores(t)
        o = matmul(p_ref[:, :trunk_len], trunk_ref[t, :lat, :], NT)
        o = o + matmul(p_ref[:, trunk_len:], branch_ref[t, :, :lat])
        o = matmul(swap, o.astype(bf16)).astype(bf16)
        lat_ref[...] = o.reshape(heads, branches, lat)
        if t == 0:
            vup_load.wait()
        for h in range(heads):
            f = matmul(lat_ref[h], vup_ref[h])
            feat_ref[0, t * branches : (t + 1) * branches, h * vdim : (h + 1) * vdim] = f.astype(bf16)
        z_first("f%d" % t, f_part(t))
        if t == 0:
            for way in (1, -1):
                w_send(way, False)

    for c in late_loads:
        c.wait()
    id_rows = ids_ref[...]
    marks = jnp.zeros((16, block), f32)
    mrow = lax.broadcasted_iota(i32, (16, block), 0)
    for e in range(EXP_DEV):
        hit = jnp.where(id_rows == ep * EXP_DEV + e, 1.0, 0.0)
        hit = jnp.sum(hit, axis=0, keepdims=True)
        marks = jnp.where(mrow == e, hit, marks)
    earlier = (ri < ci).astype(f32).astype(bf16)
    before = matmul(marks.astype(bf16), earlier)
    srow = lax.broadcasted_iota(i32, (SLOTS, block), 0).astype(f32)
    for e in range(EXP_DEV):
        chosen = (before[e : e + 1, :] == srow) & (marks[e : e + 1, :] > 0.5)
        onehot_ref[e * SLOTS : (e + 1) * SLOTS, :] = jnp.where(chosen, 1.0, 0.0).astype(bf16)

    for way in (1, -1):
        w_take(way, True)
        k = w_part(way, True)
        copy(("w2", way), w_rows(xj(-way), k), w_rows(xj(2), k), at(dx=way))
    z_second("f0", f_part(0))
    for way in (1, -1):
        w_take(way, False)
        w = w_rows(xj(-way))
        copy(("ws", way), w, w, at(flip=True))
    for t in range(1, trees):
        z_second("f%d" % t, f_part(t))

    rb_ref[j] = rt_ref[j]
    for k in range(1, GROUP):
        arrived(("r", k), rb_ref.at[(j + GROUP - k) % GROUP])
    residual = jnp.concatenate(
        [
            rb_ref[((x + d + NX) % NX) * 2 + c].astype(f32)[:, :cols]
            for d in ORDER
            for c in range(2)
        ],
        axis=1,
    )
    sum_ref[...] = residual

    own_w.wait()
    for d in (0, 1, -1):
        arrived(("ws", d), w_rows(xj_other(-d)))

    def tree_rows(t):
        return slice(t * branches, (t + 1) * branches)

    cut = cz * 3 // 4 // 128 * 128
    halves = (slice(0, cut), slice(cut, cz))
    p_ids = [ids("p", t, h, d) for t in range(trees) for h in range(2) for d in range(1, ny)]
    assert p_ids[-1] - p_ids[0] == 2 * trees * (ny - 1) - 1

    def part_copy(s, t, h, d):
        i = p_ids[0] + (2 * t + h) * (ny - 1) + d - 1
        return pltpu.make_async_remote_copy(
            src_ref=part16_ref.at[s, tree_rows(t), halves[h]],
            dst_ref=got_ref.at[d - 1, tree_rows(t), halves[h]],
            send_sem=send_sem.at[i],
            recv_sem=recv_sem.at[i],
            device_id=at(dy=d),
            device_id_type=MESH,
        )

    def project(first, last, t, h):
        feats = feat_ref[first:last, tree_rows(t), :].reshape((last - first) * branches, feat)
        for lo in range(halves[h].start, halves[h].stop, 256):
            hi = min(halves[h].stop, lo + 256)
            prod = matmul(feats, w_ref[lo:hi, :], NT).reshape(last - first, branches, hi - lo)
            part_ref[first:last, tree_rows(t), lo:hi] = prod
            part16_ref[first:last, tree_rows(t), lo:hi] = prod.astype(bf16)
        for s in range(first, last):
            d = (z + REL[s] - y + 2 * ny) % ny

            @pl.when(d != 0)
            def _():
                part_copy(s, t, h, d).start()

    dz_own = (y - z + nz) % nz
    own_slot = jnp.maximum(
        0, 2 * jnp.minimum(dz_own, nz - dz_own) - 1 + (dz_own > nz // 2).astype(i32)
    )

    def take_parts(t):
        r = tree_rows(t)
        total = part_ref[own_slot, r, :]
        for d in range(1, ny):
            for h in range(2):
                arrived(("p", t, h, d), got_ref.at[d - 1, r, halves[h]])
            total = total + got_ref[d - 1, r, :].astype(f32)
        total = sum_ref[r, :] + total
        pair = 2 * cols
        hidden = total
        for at_x in range(NX):
            places = [ORDER.index((k - at_x + 1) % NX - 1) for k in range(NX)]
            turned = jnp.concatenate([total[:, p * pair : (p + 1) * pair] for p in places], axis=1)
            hidden = jnp.where(x == at_x, turned, hidden)
        h_ref[0, x, core, r, :] = hidden.astype(bf16)

    for t in range(trees):
        z_near("f%d" % t, f_part(t))
        project(0, near, t, 0)
    for t in range(trees):
        z_far("f%d" % t, f_part(t))
        project(near, nz, t, 0)
    for way in (1, -1):
        w = w_rows(xj(2), w_part(way, True))
        arrived(("w2", way), w)
        copy(("ws2", way), w, w, at(flip=True))
    for way in (1, -1):
        arrived(("ws2", way), w_rows(xj_other(2), w_part(way, True)))
    for t in range(trees):
        project(0, nz, t, 1)
    take_parts(0)

    assert trees == 2
    ca = (cz * 2 // 7) // 128 * 128
    whole = slice(0, cz)
    low, high = slice(0, ca), slice(ca, cz)
    three = ((0, 1), (1, near), (near, nz))
    two = ((0, near), (near, nz))

    def half_cols(c, way):
        cut = c.start + ((c.stop - c.start) // 128 + 1) // 2 * 128
        return c if way is None else slice(c.start, cut) if way > 0 else slice(cut, c.stop)

    def x_at(dx):
        return (x + dx + NX) % NX

    class Region:
        def __init__(self, name, t, c, groups):
            self.name, self.r, self.c, self.groups = name, tree_rows(t), c, groups

        def own(self, s, way):
            return h_ref.at[s, x, core, self.r, half_cols(self.c, way)]

        def every_x(self, s, way):
            return h_ref.at[s, :, core, self.r, half_cols(self.c, way)]

        def one_x(self, g, dx):
            lo, hi = self.groups[g]
            return h_ref.at[lo:hi, x_at(dx), core, self.r, self.c]

        def all_x(self, g, cc):
            lo, hi = self.groups[g]
            return h_ref.at[lo:hi, :, cc, self.r, self.c]

        def x_send(self, g):
            for d in (2, 1, -1):
                copy((self.name, "x", g, d), self.one_x(g, 0), self.one_x(g, 0), at(dx=d))

        def x_take(self, g):
            for d in (1, -1, 2):
                arrived((self.name, "x", g, d), self.one_x(g, -d))

        def share(self, g):
            copy((self.name, "s", g), self.all_x(g, core), self.all_x(g, core), at(flip=True))

        def shared(self, g):
            arrived((self.name, "s", g), self.all_x(g, 1 - core))

    ra = Region("a", 0, whole, three)
    rc = Region("c", 1, low, two)
    rb = Region("b", 1, high, three)
    z_first("az", ra.own)
    ra.x_send(0)
    take_parts(1)
    rb.x_send(0)
    z_first("cz", rc.own)
    z_second("az", ra.own)
    z_near("az", ra.own)
    ra.x_send(1)
    rb.x_take(0)
    z_first("bz", rb.every_x)
    rb.share(0)
    z_second("cz", rc.own)
    z_near("cz", rc.own)
    rc.x_send(0)
    z_far("az", ra.own)
    ra.x_send(2)
    ra.x_take(0)
    ra.share(0)
    ra.x_take(1)
    ra.share(1)
    z_second("bz", rb.every_x)
    z_near("bz", rb.every_x)
    rb.share(1)
    z_far("cz", rc.own)
    rc.x_send(1)
    rc.x_take(0)
    rc.share(0)
    ra.x_take(2)
    ra.share(2)

    def pick(first, last, squares):
        for s in range(first, last):
            got = matmul(onehot_ref[...], h_ref[s].reshape(block, cz))
            picked_ref[s] = got
            squares = squares + jnp.sum(got * got, axis=-1, keepdims=True)
        return squares

    for g in range(2):
        ra.shared(g)
        rb.shared(g)
    rc.shared(0)
    squares = pick(0, near, jnp.zeros((EXP_DEV * SLOTS, 1), f32))

    si = lax.broadcasted_iota(i32, (cols, cz), 0)
    sc = lax.broadcasted_iota(i32, (cols, cz), 1)
    mine = (sc == si + j * cols).astype(f32).astype(bf16)
    hid_ref[...] = matmul(mine, h_ref[0].reshape(block, cz), NT).astype(bf16)
    results = [pltpu.make_async_copy(hid_ref, hid_hbm, out_sem.at[nz])]
    results[0].start()

    rc.x_take(1)
    rc.share(1)
    z_far("bz", rb.every_x)
    rb.share(2)
    ra.shared(2)
    rc.shared(1)
    rb.shared(2)
    squares = pick(near, nz, squares)
    scale = lax.rsqrt(squares / width + norm_eps)
    for s in range(nz):
        at_z = pl.ds(pl.multiple_of(((z + REL[s] + nz) % nz) * cz, 128), cz)
        out_ref[s] = (picked_ref[s] * scale * gain_ref[:, at_z]).astype(bf16)
        results.append(pltpu.make_async_copy(out_ref.at[s], out_hbm.at[:, at_z], out_sem.at[s]))
        results[-1].start()

    for t in range(trees):
        for h in range(2):
            for d in range(1, ny):
                part_copy(0, t, h, d).wait_send()
    for c in results:
        c.wait()
    for c in sends:
        c.wait_send()
    assert len(ids.names) <= sem_count


def hand_over(hid_in, rows_in, hid_out, rows_out, hid_ref, rows_ref, in_sem, out_sem):
    pieces = rows_in.shape[0] // SLOTS
    moves = []
    for i in range(pieces):
        r = slice(i * SLOTS, (i + 1) * SLOTS)
        moves.append((rows_in.at[r], rows_ref.at[r], rows_out.at[r]))
    moves.append((hid_in, hid_ref, hid_out))
    ins = [pltpu.make_async_copy(m[0], m[1], in_sem.at[i]) for i, m in enumerate(moves)]
    outs = [pltpu.make_async_copy(m[1], m[2], out_sem.at[i]) for i, m in enumerate(moves)]
    for c in ins:
        c.start()
    for c, o in zip(ins, outs):
        c.wait()
        o.start()
    for o in outs:
        o.wait()


def shards(
    queries,
    trunk_cache,
    branch_cache,
    visible,
    branch_len,
    value_up,
    out_proj,
    residual_in,
    norm_gain,
    expert_ids,
):
    ny = lax.axis_size("narrow")
    nz = lax.axis_size("ep") // GROUP
    trees, branches = branch_len.shape
    heads, lat, vdim = value_up.shape
    kdim = queries.shape[2]
    trunk_len = trunk_cache.shape[1]
    nkeys = branches * branch_cache.shape[2]
    feat, cols = out_proj.shape
    block = residual_in.shape[0]
    toks = trees * branches
    rows = branches * heads
    cz = GROUP * cols
    width = nz * cz
    bf16, f32 = jnp.bfloat16, jnp.float32
    sem_count = 160
    hbm = pl.BlockSpec(memory_space=pl.ANY)
    chosen = EXP_DEV * SLOTS
    hidden, rows_out = pl.pallas_call(
        functools.partial(kernel, (ny, nz, sem_count)),
        out_shape=(
            jax.ShapeDtypeStruct((cols, block), bf16),
            jax.ShapeDtypeStruct((chosen, width), bf16),
        ),
        in_specs=[hbm] * 10,
        out_specs=(hbm, hbm),
        scratch_shapes=[
            pltpu.VMEM((trees, rows, kdim), bf16),
            pltpu.VMEM((trees, kdim, trunk_len), bf16),
            pltpu.VMEM((trees, nkeys, kdim), bf16),
            pltpu.VMEM((heads, lat, vdim), bf16),
            pltpu.VMEM(visible.shape, jnp.int32),
            pltpu.VMEM(branch_len.shape, jnp.int32),
            pltpu.VMEM((cols, block), bf16),
            pltpu.VMEM((1, width), f32),
            pltpu.VMEM(expert_ids.shape[::-1], jnp.int32),
            pltpu.VMEM((rows, trunk_len + nkeys), f32),
            pltpu.VMEM((rows, trunk_len + nkeys), bf16),
            pltpu.VMEM((trees, branches, nkeys), f32),
            pltpu.VMEM((heads, branches, lat), bf16),
            pltpu.VMEM((nz, toks, feat), bf16),
            pltpu.VMEM((cz, feat), bf16),
            pltpu.VMEM((GROUP, toks, 128), bf16),
            pltpu.VMEM((GROUP, toks, 128), bf16),
            pltpu.VMEM((nz, toks, cz), f32),
            pltpu.VMEM((nz, toks, cz), bf16),
            pltpu.VMEM((ny - 1, toks, cz), bf16),
            pltpu.VMEM((toks, cz), f32),
            pltpu.VMEM((nz, NX, 2, toks, cz), bf16),
            pltpu.VMEM((chosen, block), bf16),
            pltpu.VMEM((nz, chosen, cz), f32),
            pltpu.VMEM((cols, block), bf16),
            pltpu.VMEM((nz, chosen, cz), bf16),
            pltpu.SemaphoreType.DMA((nz + 1,)),
            pltpu.SemaphoreType.DMA((16,)),
            pltpu.SemaphoreType.DMA((sem_count,)),
            pltpu.SemaphoreType.DMA((sem_count,)),
        ],
        compiler_params=pltpu.CompilerParams(
            collective_id=0, has_side_effects=True, vmem_limit_bytes=63 * 1024 * 1024
        ),
        name="decode_layer",
    )(
        queries.reshape(trees, rows, kdim),
        jnp.swapaxes(trunk_cache, 1, 2),
        branch_cache.reshape(trees, nkeys, kdim),
        value_up,
        out_proj.T,
        visible,
        branch_len,
        residual_in.T,
        norm_gain.reshape(1, width),
        expert_ids.T,
    )
    hidden, rows_out = pl.pallas_call(
        hand_over,
        out_shape=(
            jax.ShapeDtypeStruct(hidden.shape, bf16),
            jax.ShapeDtypeStruct(rows_out.shape, bf16),
        ),
        in_specs=[hbm] * 2,
        out_specs=(hbm, hbm),
        scratch_shapes=[
            pltpu.VMEM(hidden.shape, bf16),
            pltpu.VMEM(rows_out.shape, bf16),
            pltpu.SemaphoreType.DMA((EXP_DEV + 1,)),
            pltpu.SemaphoreType.DMA((EXP_DEV + 1,)),
        ],
        compiler_params=pltpu.CompilerParams(vmem_limit_bytes=63 * 1024 * 1024),
        name="hand_over",
    )(hidden, rows_out)
    return hidden.T, rows_out.reshape(1, EXP_DEV, SLOTS, width)


def solution(mesh):
    placed = (
        P("ep", "narrow", None),
        P("ep", None, None),
        P("ep", None, None, None),
        P("ep", None, None),
        P("ep", None),
        P("narrow", None, None),
        P("narrow", "ep"),
        P("narrow", "ep"),
        P(),
        P("narrow", None),
    )
    return jax.shard_map(
        shards,
        mesh=mesh,
        in_specs=placed,
        out_specs=(P("narrow", "ep"), P("narrow", "ep", None, None)),
        check_vma=False,
    )
```
